512 devices in a mesh: ctx: 64 (over z_lo, x, y), tp: 8 (over z_hi, core).
Axes of the slice: x: 4, y: 4, z: 16 (z_hi: 4, z_lo: 4; z = z_hi * 4 + z_lo), core: 2. Of those that a mesh axis runs over, the one named last changes fastest.
Arguments:
- queries: bfloat16 [8192, 32, 128], P('ctx', 'tp'), may hold values from -16.25 to 16.25
- keys: bfloat16 [8192, 8, 128], P('ctx', 'tp'), may hold values from -4 to 4
- values: bfloat16 [8192, 8, 128], P('ctx', 'tp'), may hold values from -6 to 6
- grad_out: bfloat16 [8192, 32, 128], P('ctx', 'tp'), may hold values from -6 to 6
- saved_stats: float32 [2, 32, 8192], P(None, 'tp', 'ctx'), may hold values from -4608 to 4608, as said below
- positions: int32 [8192], P('ctx'), may hold values from 0 to 8191, as said below
Outputs:
- grad_queries: bfloat16 [8192, 32, 128], P('ctx', 'tp')
- grad_keys: bfloat16 [8192, 8, 128], P('ctx', 'tp')
- grad_values: bfloat16 [8192, 8, 128], P('ctx', 'tp')
The draws below stay inside these ranges and needn't reach their ends.
Inputs may be any that keep to these rules, and one draw needn't show every extreme that they name: positions holds every number of 0 to 8191 once. It is made of 128 runs of 64 consecutive rising values: for d from 0 to 63, rows d * 128 to d * 128 + 63 hold the run starting at p(d) * 64, and the next 64 rows the run starting at (127 - p(d)) * 64, where p is a permutation of 0 to 63. saved_stats holds the forward pass's statistics for these queries, keys, values, grad_out and positions.
All inputs are finite; a program needn't handle non-finite values.
Results may differ from the reference program's by a relative error of at most 0.0075.
Values may be sent and summed in bfloat16 or wider, within the bound.
A program may use at most 64 MiB of HBM per device.

```python
import math
import jax
import jax.numpy as jnp
from jax import lax

HQ = 32
HK = 8
DH = 128
SPAN = 64
LENGTH = 8192


def draw_queries(key, part):
    key = jax.random.fold_in(key, 7)
    sample = jax.random.truncated_normal(key, -4.0, 4.0, (LENGTH, HQ, DH), jnp.float32)
    return sample.astype(jnp.bfloat16)


def draw_keys(key, part):
    key = jax.random.fold_in(key, 9)
    sample = jax.random.truncated_normal(key, -4.0, 4.0, (LENGTH, HK, DH), jnp.float32)
    return sample.astype(jnp.bfloat16)


def draw_values(key, part):
    key = jax.random.fold_in(key, 11)
    sample = jax.random.truncated_normal(key, -6.0, 6.0, (LENGTH, HK, DH), jnp.float32)
    return sample.astype(jnp.bfloat16)


def draw_grad_out(key, part):
    key = jax.random.fold_in(key, 13)
    sample = jax.random.truncated_normal(key, -6.0, 6.0, (LENGTH, HQ, DH), jnp.float32)
    return sample.astype(jnp.bfloat16)


def draw_positions(key, part):
    key = jax.random.fold_in(key, 5)
    devices = LENGTH // (2 * SPAN)
    device_order = jax.random.permutation(key, devices).astype(jnp.int32)
    run_ids = jnp.stack([device_order, 2 * devices - 1 - device_order], axis=1).reshape(2 * devices)
    offsets = jnp.arange(SPAN, dtype=jnp.int32)
    return (run_ids[:, None] * SPAN + offsets[None, :]).reshape(LENGTH).astype(jnp.int32)


def forward_stats(queries, keys, values, grad_out, positions):
    softmax_scale = 1.0 / math.sqrt(DH)
    group_size = HQ // HK
    block_rows = LENGTH // 16
    block_count = LENGTH // block_rows

    def one_head(head_index):
        key_rows = lax.dynamic_index_in_dim(keys, head_index, 1, keepdims=False)
        value_rows = lax.dynamic_index_in_dim(values, head_index, 1, keepdims=False).astype(jnp.float32)
        query_rows = lax.dynamic_slice_in_dim(queries, head_index * group_size, group_size, 1)
        grad_rows = lax.dynamic_slice_in_dim(grad_out, head_index * group_size, group_size, 1)

        def query_block(carried, block_index):
            row_start = (block_index * block_rows).astype(jnp.int32)
            query_part = lax.dynamic_slice_in_dim(query_rows, row_start, block_rows, 0)
            query_part = query_part.transpose(1, 0, 2).reshape(group_size * block_rows, DH)
            grad_part = lax.dynamic_slice_in_dim(grad_rows, row_start, block_rows, 0)
            grad_part = grad_part.transpose(1, 0, 2).reshape(group_size * block_rows, DH).astype(jnp.float32)
            pos_part = jnp.tile(lax.dynamic_slice_in_dim(positions, row_start, block_rows, 0), group_size)
            scores = jnp.dot(query_part, key_rows.T, preferred_element_type=jnp.float32) * softmax_scale
            visible = positions[None, :] <= pos_part[:, None]
            scores = jnp.where(visible, scores, -1e+30)
            row_max = jnp.max(scores, axis=1)
            weight = jnp.exp(scores - row_max[:, None])
            total = jnp.sum(weight, axis=1)
            output = jnp.dot(weight / total[:, None], value_rows, precision=lax.Precision.HIGHEST)
            delta = jnp.sum(grad_part * output, axis=1)
            return (carried, jnp.stack([row_max + jnp.log(total), delta]))
        unused, stats = lax.scan(query_block, jnp.zeros((), jnp.float32), jnp.arange(block_count, dtype=jnp.int32))
        return stats.reshape(block_count, 2, group_size, block_rows).transpose(1, 2, 0, 3).reshape(2, group_size, LENGTH)
    stats = lax.map(one_head, jnp.arange(HK, dtype=jnp.int32))
    return stats.transpose(1, 0, 2, 3).reshape(2, HQ, LENGTH)


def draw_saved_stats(key, part):
    queries = draw_queries(key, part)
    keys = draw_keys(key, part)
    values = draw_values(key, part)
    grad_out = draw_grad_out(key, part)
    positions = draw_positions(key, part)
    return forward_stats(queries, keys, values, grad_out, positions).astype(jnp.float32)


def setup_inputs(seed: int = 0) -> dict:
    key_of = jax.random.split(jax.random.key(seed), 7)
    return {
        "queries": draw_queries(jax.random.fold_in(key_of[6], 71), 0),
        "keys": draw_keys(jax.random.fold_in(key_of[6], 71), 0),
        "values": draw_values(jax.random.fold_in(key_of[6], 71), 0),
        "grad_out": draw_grad_out(jax.random.fold_in(key_of[6], 71), 0),
        "saved_stats": draw_saved_stats(jax.random.fold_in(key_of[6], 71), 0),
        "positions": draw_positions(jax.random.fold_in(key_of[6], 71), 0),
    }


masked_score = -1e+30

def reference(queries, keys, values, grad_out, saved_stats, positions):
    softmax_scale = 1.0 / math.sqrt(DH)
    group_size = HQ // HK
    block_rows = LENGTH // 16
    block_count = LENGTH // block_rows

    def one_head(head_index):
        key_rows = lax.dynamic_index_in_dim(keys, head_index, 1, keepdims=False)
        value_rows = lax.dynamic_index_in_dim(values, head_index, 1, keepdims=False)
        query_rows = lax.dynamic_slice_in_dim(queries, head_index * group_size, group_size, 1)
        grad_rows = lax.dynamic_slice_in_dim(grad_out, head_index * group_size, group_size, 1)

        def query_block(carried, block_index):
            key_sum, value_sum = carried
            row_start = (block_index * block_rows).astype(jnp.int32)
            query_part = lax.dynamic_slice_in_dim(query_rows, row_start, block_rows, 0)
            query_part = query_part.transpose(1, 0, 2).reshape(group_size * block_rows, DH)
            grad_part = lax.dynamic_slice_in_dim(grad_rows, row_start, block_rows, 0)
            grad_part = grad_part.transpose(1, 0, 2).reshape(group_size * block_rows, DH)
            pos_part = jnp.tile(lax.dynamic_slice_in_dim(positions, row_start, block_rows, 0), group_size)
            stat_part = lax.dynamic_slice(saved_stats, (jnp.zeros((), jnp.int32), (head_index * group_size).astype(jnp.int32), row_start), (2, group_size, block_rows))
            stat_part = stat_part.reshape(2, group_size * block_rows)
            scores = jnp.dot(query_part, key_rows.T, preferred_element_type=jnp.float32) * softmax_scale
            visible = positions[None, :] <= pos_part[:, None]
            probs = jnp.exp(jnp.where(visible, scores - stat_part[0][:, None], masked_score))
            grad_probs = jnp.dot(grad_part, value_rows.T, preferred_element_type=jnp.float32)
            grad_scores = (probs * (grad_probs - stat_part[1][:, None])).astype(jnp.bfloat16)
            grad_query = jnp.dot(grad_scores, key_rows, preferred_element_type=jnp.float32) * softmax_scale
            key_sum = key_sum + jnp.dot(grad_scores.T, query_part, preferred_element_type=jnp.float32)
            value_sum = value_sum + jnp.dot(probs.astype(jnp.bfloat16).T, grad_part, preferred_element_type=jnp.float32)
            return ((key_sum, value_sum), grad_query.astype(jnp.bfloat16).reshape(group_size, block_rows, DH))
        zero_sum = jnp.zeros((LENGTH, DH), jnp.float32)
        sums, grad_query = lax.scan(query_block, (zero_sum, zero_sum), jnp.arange(block_count, dtype=jnp.int32))
        grad_query = grad_query.transpose(0, 2, 1, 3).reshape(LENGTH, group_size, DH)
        return (grad_query, (sums[0] * softmax_scale).astype(jnp.bfloat16), sums[1].astype(jnp.bfloat16))
    grad_query, grad_key, grad_value = lax.map(one_head, jnp.arange(HK, dtype=jnp.int32))
    grad_queries = grad_query.transpose(1, 0, 2, 3).reshape(LENGTH, HQ, DH)
    return (grad_queries, grad_key.transpose(1, 0, 2), grad_value.transpose(1, 0, 2))
```

```python
import math

import jax
import jax.numpy as jnp
from jax import lax
from jax.experimental import pallas as pl
from jax.experimental.pallas import tpu as pltpu
from jax.sharding import PartitionSpec as P

SIDE = 4
SPAN = 64
DIM = 128
GROUP = 4
ROWS = SPAN * GROUP
KEYS = SPAN * SIDE
LOG2E = 1.4426950408889634
SCALE = 1.0 / math.sqrt(DIM)
F32 = jnp.float32
BF16 = jnp.bfloat16
MESH = pl.DeviceIdType.MESH


def dot_nt(a, b):
    return lax.dot_general(a, b, (((1,), (1,)), ((), ())), preferred_element_type=F32)


def dot_nn(a, b):
    return jnp.dot(a, b, preferred_element_type=F32)


class Links:
    def __init__(self, send_sems, recv_sems):
        self.send_sems = send_sems
        self.recv_sems = recv_sems
        self.count = 0
        self.made = []

    def copy(self, src, dst, device):
        made = pltpu.make_async_remote_copy(
            src_ref=src,
            dst_ref=dst,
            send_sem=self.send_sems.at[self.count],
            recv_sem=self.recv_sems.at[self.count],
            device_id={"ctx": device},
            device_id_type=MESH,
        )
        self.count += 1
        self.made.append(made)
        return made


def kernel(
    q_in, k_in, v_in, g_in, st_in, pos_in,
    dq_out, dk_out, dv_out,
    qd, kv, meta, stats, pos, kt, acc, dqt,
    part, relay, ybuf, zpart, zbuf, xpart, xrelay, xbuf,
    local_sems, send_sems, recv_sems,
):
    me = lax.axis_index("ctx")
    z, x, y = me // (SIDE * SIDE), (me // SIDE) % SIDE, me % SIDE

    def at(dz=0, dx=0, dy=0):
        return (
            ((z + dz) % SIDE) * (SIDE * SIDE) + ((x + dx) % SIDE) * SIDE + (y + dy) % SIDE
        )

    peers = [at(dx=1), at(dx=2), at(dx=3), at(dy=1), at(dy=3), at(dz=1), at(dz=2), at(dz=3)]

    loads = [
        pltpu.make_async_copy(q_in, qd.at[0, 0], local_sems.at[0]),
        pltpu.make_async_copy(g_in, qd.at[0, 1], local_sems.at[1]),
        pltpu.make_async_copy(k_in, kv.at[0, pl.ds(0, 128)], local_sems.at[2]),
        pltpu.make_async_copy(v_in, kv.at[0, pl.ds(128, 128)], local_sems.at[3]),
        pltpu.make_async_copy(st_in, stats, local_sems.at[4]),
        pltpu.make_async_copy(pos_in, pos, local_sems.at[5]),
    ]
    for load in loads:
        load.start()
    barrier = pltpu.get_barrier_semaphore()
    for peer in peers:
        pl.semaphore_signal(barrier, inc=1, device_id={"ctx": peer}, device_id_type=MESH)

    for load in loads:
        load.wait()
    span = (pos[0:1, 0:1] // SPAN).astype(F32)
    kv[0, 256:272, :] = jnp.broadcast_to(span, (16, DIM)).astype(BF16)
    spread_t = lax.broadcasted_iota(jnp.int32, (128, 512), 0)
    spread_r = lax.broadcasted_iota(jnp.int32, (128, 512), 1)
    spread = jnp.where(spread_r // GROUP == spread_t, 1.0, 0.0).astype(F32)
    wide = jnp.dot(
        stats[...], spread, preferred_element_type=F32, precision=lax.Precision.HIGHEST
    )
    head_of = lax.broadcasted_iota(jnp.int32, (8, 512), 0) % GROUP
    lane_of = lax.broadcasted_iota(jnp.int32, (8, 512), 1) % GROUP
    wide = jnp.where(head_of == lane_of, wide, 0.0)
    meta[0, 0:1, :] = jnp.sum(wide[0:4], axis=0, keepdims=True) * LOG2E
    meta[0, 1:2, :] = jnp.sum(wide[4:8], axis=0, keepdims=True)
    meta[0, 2:3, :] = jnp.broadcast_to(span, (1, 512))
    meta[0, 3:8, :] = jnp.zeros((5, 512), F32)

    pl.semaphore_wait(barrier, len(peers))

    links = Links(send_sems, recv_sems)
    q_right = links.copy(qd.at[0, 0], qd.at[3, 0], at(dx=1))
    g_left = links.copy(qd.at[0, 1], qd.at[1, 1], at(dx=3))
    g_right = links.copy(qd.at[0, 1], qd.at[3, 1], at(dx=1))
    q_left = links.copy(qd.at[0, 0], qd.at[1, 0], at(dx=3))
    q_on = links.copy(qd.at[3, 0], qd.at[2, 0], at(dx=1))
    g_on = links.copy(qd.at[1, 1], qd.at[2, 1], at(dx=3))
    meta_go = [links.copy(meta.at[0], meta.at[SIDE - s], at(dx=s)) for s in range(1, SIDE)]
    z_go = [
        links.copy(kv.at[0], kv.at[SIDE * (SIDE - s)], at(dz=s)) for s in range(1, SIDE)
    ]
    y_go = []
    for c in range(SIDE):
        k_part, v_part = pl.ds(0, 128), pl.ds(128, 144)
        b = SIDE * c
        y_go.append(
            dict(
                k_right=links.copy(kv.at[b, k_part], kv.at[b + 3, k_part], at(dy=1)),
                v_left=links.copy(kv.at[b, v_part], kv.at[b + 1, v_part], at(dy=3)),
                v_right=links.copy(kv.at[b, v_part], kv.at[b + 3, v_part], at(dy=1)),
                k_left=links.copy(kv.at[b, k_part], kv.at[b + 1, k_part], at(dy=3)),
                k_on=links.copy(kv.at[b + 3, k_part], kv.at[b + 2, k_part], at(dy=1)),
                v_on=links.copy(kv.at[b + 1, v_part], kv.at[b + 2, v_part], at(dy=3)),
            )
        )
    r_go = []
    k_rows, v_rows = pl.ds(0, 128), pl.ds(128, 128)
    for c in range(SIDE):
        r_go.append(
            dict(
                k_relay=links.copy(part.at[c, 1, k_rows], relay.at[c, 0], at(dy=1)),
                v_relay=links.copy(part.at[c, 1, v_rows], relay.at[c, 1], at(dy=3)),
                v_right=links.copy(part.at[c, 0, v_rows], ybuf.at[c, 0, v_rows], at(dy=1)),
                k_left=links.copy(part.at[c, 2, k_rows], ybuf.at[c, 1, k_rows], at(dy=3)),
                k_right=links.copy(part.at[c, 0, k_rows], ybuf.at[c, 0, k_rows], at(dy=1)),
                v_left=links.copy(part.at[c, 2, v_rows], ybuf.at[c, 1, v_rows], at(dy=3)),
            )
        )
    rz_go = [None] + [links.copy(zpart.at[s - 1], zbuf.at[s - 1], at(dz=s)) for s in range(1, SIDE)]
    dq_go = dict(
        e_relay=links.copy(xpart.at[1, k_rows], xrelay.at[0], at(dx=1)),
        l_relay=links.copy(xpart.at[1, v_rows], xrelay.at[1], at(dx=3)),
        l_right=links.copy(xpart.at[0, v_rows], xbuf.at[0, v_rows], at(dx=1)),
        e_left=links.copy(xpart.at[2, k_rows], xbuf.at[1, k_rows], at(dx=3)),
        e_right=links.copy(xpart.at[0, k_rows], xbuf.at[0, k_rows], at(dx=1)),
        l_left=links.copy(xpart.at[2, v_rows], xbuf.at[1, v_rows], at(dx=3)),
    )

    for s in range(SIDE - 1):
        z_go[s].start()
    for copy in (q_right, g_left):
        copy.start()
    for name in ("k_right", "v_left", "v_right", "k_left"):
        y_go[0][name].start()
    for copy in meta_go:
        copy.start()
    for copy in (g_right, q_left):
        copy.start()

    acc[...] = jnp.zeros_like(acc)
    dqt[...] = jnp.zeros_like(dqt)

    for c in range(1, SIDE):
        z_go[SIDE - 1 - c].wait_recv()
        for name in ("k_right", "v_left", "v_right", "k_left"):
            y_go[c][name].start()
    q_right.wait_recv()
    q_on.start()
    g_left.wait_recv()
    g_on.start()
    for c in range(SIDE):
        y_go[c]["k_right"].wait_recv()
        y_go[c]["k_on"].start()
        y_go[c]["v_left"].wait_recv()
        y_go[c]["v_on"].start()

    def probs_of(scores, log_total):
        return jnp.exp2(scores * (SCALE * LOG2E) - log_total)

    def own_early():
        key, value = kv[0, 0:64, :], kv[0, 128:192, :]
        query, grad = qd[0, 0, 0:ROWS, :], qd[0, 1, 0:ROWS, :]
        row_k = lax.broadcasted_iota(jnp.int32, (SPAN, ROWS), 0)
        col_r = lax.broadcasted_iota(jnp.int32, (SPAN, ROWS), 1) // GROUP
        scores = dot_nt(key, query) * (SCALE * LOG2E) - meta[0, 0:1, 0:ROWS]
        probs = jnp.exp2(jnp.where(row_k <= col_r, scores, -1e30))
        grad_probs = dot_nt(value, grad)
        grad_scores = (probs * (grad_probs - meta[0, 1:2, 0:ROWS])).astype(BF16)
        acc[0, 128:192, :] += dot_nn(probs.astype(BF16), grad)
        acc[0, 0:64, :] += dot_nn(grad_scores, query)
        dqt[0, 0:128, :] += dot_nn(key.T, grad_scores)

    def step(d, c, own):
        base = SIDE * c
        slots = pl.ds(base, SIDE)

        def rows(start):
            return kv[slots, start : start + SPAN, :].reshape(KEYS, DIM)

        k_e, k_l, v_e, v_l = rows(0), rows(64), rows(128), rows(192)
        q_e, q_l = qd[d, 0, 0:ROWS, :], qd[d, 0, ROWS : 2 * ROWS, :]
        g_e, g_l = qd[d, 1, 0:ROWS, :], qd[d, 1, ROWS : 2 * ROWS, :]
        lse_e, lse_l = meta[d, 0:1, 0:ROWS], meta[d, 0:1, ROWS : 2 * ROWS]
        del_e, del_l = meta[d, 1:2, 0:ROWS], meta[d, 1:2, ROWS : 2 * ROWS]
        span_k = kv[slots, 256:272, :].astype(F32)[:, 0:1, :]
        span_q = meta[d, 2:3, 0:DIM]
        low = jnp.where(span_k < span_q[None], 1.0, 0.0)
        low_rows = jnp.broadcast_to(low, (SIDE, SPAN, DIM)).reshape(KEYS, DIM)
        high_rows = 1.0 - low_rows
        low_wide = jnp.concatenate([low, low], axis=2)
        lane_block = lax.broadcasted_iota(jnp.int32, (1, KEYS), 1) // SPAN
        low_lane = jnp.zeros((1, KEYS), F32)
        for e in range(SIDE):
            low_lane = jnp.where(lane_block == e, low_wide[e], low_lane)

        @pl.when(d == 0)
        def _():
            kt[c, 0:128, :] = k_e.T
            kt[c, 128:256, :] = k_l.T

        probs = probs_of(dot_nt(k_e, q_l), lse_l)
        grad_probs = dot_nt(v_e, g_l)
        grad_scores = (probs * (grad_probs - del_l)).astype(BF16)
        dv_e = dot_nn(probs.astype(BF16), g_l)
        dk_e = dot_nn(grad_scores, q_l)
        dq_l = dot_nn(kt[c, 0:128, :], grad_scores)

        low_b, high_b = low_rows.astype(BF16), high_rows.astype(BF16)
        k_cat = jnp.concatenate([k_e * low_b, k_l * high_b], axis=1)
        v_cat = jnp.concatenate([v_e * low_b, v_l * high_b], axis=1)
        q_cat = jnp.concatenate([q_e, q_l], axis=1)
        g_cat = jnp.concatenate([g_e, g_l], axis=1)
        lse = jnp.where(low_wide > 0.5, lse_e[None], lse_l[None])
        delta = jnp.where(low_wide > 0.5, del_e[None], del_l[None])
        scores = dot_nt(k_cat, q_cat).reshape(SIDE, SPAN, ROWS) * (SCALE * LOG2E) - lse
        row_k = lax.broadcasted_iota(jnp.int32, (SPAN, ROWS), 0)
        col_r = lax.broadcasted_iota(jnp.int32, (SPAN, ROWS), 1) // GROUP
        seen = row_k <= col_r + jnp.where(own, 0, SPAN)
        first = jnp.where(seen, scores[0], -1e30)
        scores = jnp.concatenate([first[None], scores[1:]], axis=0)
        probs = jnp.exp2(scores)
        grad_probs = dot_nt(v_cat, g_cat).reshape(SIDE, SPAN, ROWS)
        grad_scores = (probs * (grad_probs - delta)).astype(BF16).reshape(KEYS, ROWS)
        probs = probs.astype(BF16).reshape(KEYS, ROWS)
        dv = dot_nn(probs, g_cat)
        dk = dot_nn(grad_scores, q_cat)
        low_lane_b, high_lane_b = low_lane.astype(BF16), (1.0 - low_lane).astype(BF16)
        kt_cat = jnp.concatenate(
            [kt[c, 0:128, :] * low_lane_b, kt[c, 128:256, :] * high_lane_b], axis=0
        )
        dq = dot_nn(kt_cat, grad_scores)

        def add(start, value):
            acc[slots, start : start + SPAN, :] += value.reshape(SIDE, SPAN, DIM)

        add(0, dk_e + dk[:, 0:128] * low_rows)
        add(64, dk[:, 128:256] * high_rows)
        add(128, dv_e + dv[:, 0:128] * low_rows)
        add(192, dv[:, 128:256] * high_rows)
        dqt[d, 0:128, :] += dq[0:128]
        dqt[d, 128:256, :] += dq[128:256] + dq_l

    def send_y(c):
        b = SIDE * c
        part[c, 1] = acc[b + 2].astype(BF16)
        r_go[c]["k_relay"].start()
        r_go[c]["v_relay"].start()
        part[c, 0, 128:256] = acc[b + 1, 128:256].astype(BF16)
        r_go[c]["v_right"].start()
        part[c, 2, 0:128] = acc[b + 3, 0:128].astype(BF16)
        r_go[c]["k_left"].start()

    def relay_y(c):
        b = SIDE * c
        r_go[c]["k_relay"].wait_recv()
        part[c, 0, 0:128] = (acc[b + 1, 0:128] + relay[c, 0].astype(F32)).astype(BF16)
        r_go[c]["k_right"].start()
        r_go[c]["v_relay"].wait_recv()
        part[c, 2, 128:256] = (acc[b + 3, 128:256] + relay[c, 1].astype(F32)).astype(BF16)
        r_go[c]["v_left"].start()

    def sum_y(c):
        for name in ("v_right", "k_left", "k_right", "v_left"):
            r_go[c][name].wait_recv()
        return acc[SIDE * c] + ybuf[c, 0].astype(F32) + ybuf[c, 1].astype(F32)

    def send_z(c):
        zpart[c - 1] = sum_y(c).astype(BF16)
        rz_go[c].start()

    def loop_step(i, carry):
        j = i - SIDE
        m = j % 3
        c = jnp.where(i < SIDE, i, (j // 3 + 1) % SIDE)
        d = jnp.where(i < SIDE, 0, 2 - m + 3 * (m // 2))

        def before(n):
            return pl.when(i == n)

        for n in range(SIDE):

            @before(n)
            def _(n=n):
                if n == 0:
                    y_go[n]["v_right"].wait_recv()
                    y_go[n]["k_left"].wait_recv()
                    y_go[n]["k_on"].wait_recv()
                    y_go[n]["v_on"].wait_recv()
                    own_early()
                else:
                    y_go[n]["v_right"].wait_recv()
                    y_go[n]["k_left"].wait_recv()
                    y_go[n]["k_on"].wait_recv()
                    y_go[n]["v_on"].wait_recv()

        @before(SIDE)
        def _():
            for copy in [g_right, q_left, q_on, g_on] + meta_go:
                copy.wait_recv()

        step(d, c, i == 0)

        @pl.when(i == 6)
        def _():
            send_y(1)

        @pl.when(i == 9)
        def _():
            relay_y(1)
            send_y(2)

        @pl.when(i == 12)
        def _():
            send_z(1)
            relay_y(2)
            send_y(3)

        @pl.when(i == 13)
        def _():
            xpart[1] = dqt[2].astype(BF16)
            dq_go["e_relay"].start()
            dq_go["l_relay"].start()

        @pl.when(i == 14)
        def _():
            xpart[0, 128:256] = dqt[1, 128:256].astype(BF16)
            dq_go["l_right"].start()

        return carry

    lax.fori_loop(0, SIDE * SIDE, loop_step, 0)

    send_y(0)
    xpart[2, 0:128] = dqt[3, 0:128].astype(BF16)
    dq_go["e_left"].start()
    dq_go["e_relay"].wait_recv()
    xpart[0, 0:128] = (dqt[1, 0:128] + xrelay[0].astype(F32)).astype(BF16)
    dq_go["e_right"].start()
    dq_go["l_relay"].wait_recv()
    xpart[2, 128:256] = (dqt[3, 128:256] + xrelay[1].astype(F32)).astype(BF16)
    dq_go["l_left"].start()
    send_z(2)
    relay_y(3)
    send_z(3)
    relay_y(0)
    for name in ("l_right", "e_left", "e_right", "l_left"):
        dq_go[name].wait_recv()
    total = (dqt[0] + xbuf[0].astype(F32) + xbuf[1].astype(F32)) * SCALE
    dq_out[0:ROWS, :] = total[0:128].T.astype(BF16)
    dq_out[ROWS : 2 * ROWS, :] = total[128:256].T.astype(BF16)
    own = sum_y(0)
    for s in range(1, SIDE):
        rz_go[s].wait_recv()
        own = own + zbuf[s - 1].astype(F32)
    dk_out[...] = (own[0:128] * SCALE).astype(BF16)
    dv_out[...] = own[128:256].astype(BF16)
    for copy in links.made:
        copy.wait_send()


COPIES = 6 + 3 + 3 + 24 + 24 + 3 + 6


def body(queries, keys, values, grad_out, saved_stats, positions):
    any_spec = pl.BlockSpec(memory_space=pl.ANY)
    vmem_spec = pl.BlockSpec(memory_space=pltpu.VMEM)
    dq, dk, dv = pl.pallas_call(
        kernel,
        out_shape=(
            jax.ShapeDtypeStruct((512, DIM), BF16),
            jax.ShapeDtypeStruct((128, DIM), BF16),
            jax.ShapeDtypeStruct((128, DIM), BF16),
        ),
        in_specs=[any_spec] * 6,
        out_specs=(vmem_spec,) * 3,
        scratch_shapes=[
            pltpu.VMEM((4, 2, 512, DIM), BF16),
            pltpu.VMEM((16, 272, DIM), BF16),
            pltpu.VMEM((4, 8, 512), F32),
            pltpu.VMEM((8, 128), F32),
            pltpu.VMEM((1, 128), jnp.int32),
            pltpu.VMEM((4, 256, KEYS), BF16),
            pltpu.VMEM((16, 256, DIM), F32),
            pltpu.VMEM((4, 256, ROWS), F32),
            pltpu.VMEM((4, 3, 256, DIM), BF16),
            pltpu.VMEM((4, 2, 128, DIM), BF16),
            pltpu.VMEM((4, 2, 256, DIM), BF16),
            pltpu.VMEM((3, 256, DIM), BF16),
            pltpu.VMEM((3, 256, DIM), BF16),
            pltpu.VMEM((3, 256, ROWS), BF16),
            pltpu.VMEM((2, 128, ROWS), BF16),
            pltpu.VMEM((2, 256, ROWS), BF16),
            pltpu.SemaphoreType.DMA((6,)),
            pltpu.SemaphoreType.DMA((COPIES,)),
            pltpu.SemaphoreType.DMA((COPIES,)),
        ],
        compiler_params=pltpu.CompilerParams(
            collective_id=0, has_side_effects=True, vmem_limit_bytes=48 * 1024 * 1024
        ),
    )(
        queries.reshape(512, DIM),
        keys.reshape(128, DIM),
        values.reshape(128, DIM),
        grad_out.reshape(512, DIM),
        saved_stats.reshape(8, 128),
        positions.reshape(1, 128),
    )
    return dq.reshape(128, GROUP, DIM), dk.reshape(128, 1, DIM), dv.reshape(128, 1, DIM)


def solution(mesh):
    in_specs = (
        P("ctx", "tp", None),
        P("ctx", "tp", None),
        P("ctx", "tp", None),
        P("ctx", "tp", None),
        P(None, "tp", "ctx"),
        P("ctx"),
    )
    out_specs = (P("ctx", "tp", None), P("ctx", "tp", None), P("ctx", "tp", None))
    return jax.shard_map(body, mesh=mesh, in_specs=in_specs, out_specs=out_specs, check_vma=False)
```

```python
import math

import jax
import jax.numpy as jnp
from jax import lax
from jax.experimental import pallas as pl
from jax.experimental.pallas import tpu as pltpu
from jax.sharding import PartitionSpec as P

SIDE = 4
SPAN = 64
DIM = 128
GROUP = 4
ROWS = SPAN * GROUP
KEYS = SPAN * SIDE
LOG2E = 1.4426950408889634
SCALE = 1.0 / math.sqrt(DIM)
F32 = jnp.float32
BF16 = jnp.bfloat16
MESH = pl.DeviceIdType.MESH


def dot_nt(a, b):
    return lax.dot_general(a, b, (((1,), (1,)), ((), ())), preferred_element_type=F32)


def dot_tn(a, b):
    return lax.dot_general(a, b, (((0,), (0,)), ((), ())), preferred_element_type=F32)


def dot_nn(a, b):
    return jnp.dot(a, b, preferred_element_type=F32)


class Links:
    def __init__(self, send_sems, recv_sems):
        self.send_sems = send_sems
        self.recv_sems = recv_sems
        self.count = 0
        self.made = []

    def copy(self, src, dst, device):
        made = pltpu.make_async_remote_copy(
            src_ref=src,
            dst_ref=dst,
            send_sem=self.send_sems.at[self.count],
            recv_sem=self.recv_sems.at[self.count],
            device_id={"ctx": device},
            device_id_type=MESH,
        )
        self.count += 1
        self.made.append(made)
        return made


def kernel(
    q_in, k_in, v_in, g_in, st_in, pos_in,
    out,
    qd, kv, meta, stats, pos, qt, acc, dqt,
    part, ybuf, zpart, zbuf, xpart, xbuf,
    local_sems, send_sems, recv_sems,
):
    me = lax.axis_index("ctx")
    z, x, y = me // (SIDE * SIDE), (me // SIDE) % SIDE, me % SIDE

    def at(dz=0, dx=0, dy=0):
        return (
            ((z + dz) % SIDE) * (SIDE * SIDE) + ((x + dx) % SIDE) * SIDE + (y + dy) % SIDE
        )

    peers = [at(dx=1), at(dx=2), at(dx=3), at(dy=1), at(dy=2), at(dy=3), at(dz=1), at(dz=2), at(dz=3)]

    loads = [
        pltpu.make_async_copy(q_in, qd.at[0, 0], local_sems.at[0]),
        pltpu.make_async_copy(g_in, qd.at[0, 1], local_sems.at[1]),
        pltpu.make_async_copy(k_in, kv.at[0, pl.ds(0, 128)], local_sems.at[2]),
        pltpu.make_async_copy(v_in.at[pl.ds(0, 64)], kv.at[0, pl.ds(128, 64)], local_sems.at[3]),
        pltpu.make_async_copy(v_in.at[pl.ds(64, 64)], kv.at[0, pl.ds(208, 64)], local_sems.at[6]),
        pltpu.make_async_copy(st_in, stats, local_sems.at[4]),
        pltpu.make_async_copy(pos_in, pos, local_sems.at[5]),
    ]
    for load in loads:
        load.start()
    barrier = pltpu.get_barrier_semaphore()
    for peer in peers:
        pl.semaphore_signal(barrier, inc=1, device_id={"ctx": peer}, device_id_type=MESH)

    for load in loads[2:5] + loads[6:]:
        load.wait()
    span = (pos[0:1, 0:1] // SPAN).astype(F32)
    kv[0, 192:208, :] = jnp.broadcast_to(span, (16, DIM)).astype(BF16)

    links = Links(send_sems, recv_sems)
    q_go = [None] + [
        [links.copy(qd.at[0, n], qd.at[s, n], at(dx=SIDE - s)) for n in range(2)]
        for s in range(1, SIDE)
    ]
    meta_go = [None] + [
        links.copy(meta.at[0], meta.at[s], at(dx=SIDE - s)) for s in range(1, SIDE)
    ]
    z_go = [None] + [
        links.copy(kv.at[0], kv.at[SIDE * s], at(dz=SIDE - s)) for s in range(1, SIDE)
    ]
    y_go = [
        [links.copy(kv.at[SIDE * c], kv.at[SIDE * c + s], at(dy=SIDE - s)) for s in range(1, SIDE)]
        for c in range(SIDE)
    ]
    ry_go = [
        [links.copy(part.at[c, s - 1], ybuf.at[c, s - 1], at(dy=s)) for s in range(1, SIDE)]
        for c in range(SIDE)
    ]
    rz_go = [None] + [
        links.copy(zpart.at[s - 1], zbuf.at[s - 1], at(dz=s)) for s in range(1, SIDE)
    ]
    rx_go = [None] + [
        links.copy(xpart.at[s - 1], xbuf.at[s - 1], at(dx=s)) for s in range(1, SIDE)
    ]

    def start(copies):
        for copy in copies:
            copy.start()

    def arrive(copies):
        for copy in copies:
            copy.wait_recv()

    pl.semaphore_wait(barrier, len(peers))
    start((z_go[1], z_go[3], z_go[2]))
    start(y_go[0])
    for load in loads[0:2]:
        load.wait()
    start(q_go[1])
    start(q_go[3])

    loads[5].wait()
    spread_t = lax.broadcasted_iota(jnp.int32, (128, 512), 0)
    spread_r = lax.broadcasted_iota(jnp.int32, (128, 512), 1)
    spread = jnp.where(spread_r // GROUP == spread_t, 1.0, 0.0).astype(F32)
    wide = jnp.dot(
        stats[...], spread, preferred_element_type=F32, precision=lax.Precision.HIGHEST
    )
    head_of = lax.broadcasted_iota(jnp.int32, (8, 512), 0) % GROUP
    lane_of = lax.broadcasted_iota(jnp.int32, (8, 512), 1) % GROUP
    wide = jnp.where(head_of == lane_of, wide, 0.0)
    meta[0, 0:1, :] = jnp.sum(wide[0:4], axis=0, keepdims=True) * LOG2E
    meta[0, 1:2, :] = jnp.sum(wide[4:8], axis=0, keepdims=True)
    meta[0, 2:3, :] = jnp.broadcast_to(span, (1, 512))
    meta[0, 3:8, :] = jnp.zeros((5, 512), F32)
    start(meta_go[1:])

    for c in (1, 3, 2):
        arrive([z_go[c]])
        start(y_go[c])
    start(q_go[2])

    acc[...] = jnp.zeros_like(acc)
    dqt[...] = jnp.zeros_like(dqt)

    def probs_of(scores, log_total):
        return jnp.exp2(scores * (SCALE * LOG2E) - log_total)

    def turn(d):
        for n in range(2):
            qt[d, n, 0:128, :] = qd[d, n, 0:ROWS, :].T
            qt[d, n, 128:256, :] = qd[d, n, ROWS : 2 * ROWS, :].T

    def own_early():
        key, value = kv[0, 0:64, :], kv[0, 128:192, :]
        query, grad = qd[0, 0, 0:ROWS, :], qd[0, 1, 0:ROWS, :]
        row_k = lax.broadcasted_iota(jnp.int32, (SPAN, ROWS), 0)
        col_r = lax.broadcasted_iota(jnp.int32, (SPAN, ROWS), 1) // GROUP
        scores = dot_nt(key, query) * (SCALE * LOG2E) - meta[0, 0:1, 0:ROWS]
        probs = jnp.exp2(jnp.where(row_k <= col_r, scores, -1e30))
        grad_probs = dot_nt(value, grad)
        grad_scores = (probs * (grad_probs - meta[0, 1:2, 0:ROWS])).astype(BF16)
        acc[0, 128:192, :] += dot_nn(probs.astype(BF16), grad)
        acc[0, 0:64, :] += dot_nn(grad_scores, query)
        dqt[0, 0:128, :] += dot_tn(key, grad_scores)

    def step(group, c, own):
        base = SIDE * c
        slots = pl.ds(base, SIDE)

        def rows(start):
            return kv[slots, start : start + SPAN, :].reshape(KEYS, DIM)

        k_e, k_l, v_e, v_l = rows(0), rows(64), rows(128), rows(208)
        span_k = kv[slots, 192:208, :].astype(F32)[:, 0:1, :]
        st = []
        for d in group:
            q_e, q_l = qd[d, 0, 0:ROWS, :], qd[d, 0, ROWS : 2 * ROWS, :]
            g_e, g_l = qd[d, 1, 0:ROWS, :], qd[d, 1, ROWS : 2 * ROWS, :]
            span_q = meta[d, 2:3, 0:DIM]
            low = jnp.where(span_k < span_q[None], 1.0, 0.0)
            low_rows = jnp.broadcast_to(low, (SIDE, SPAN, DIM)).reshape(KEYS, DIM)
            high_rows = 1.0 - low_rows
            low_wide = jnp.concatenate([low, low], axis=2)
            low_b, high_b = low_rows.astype(BF16), high_rows.astype(BF16)
            k_cat = jnp.concatenate([k_e * low_b, k_l * high_b], axis=1)
            v_cat = jnp.concatenate([v_e * low_b, v_l * high_b], axis=1)
            s1 = dot_nn(k_e, qt[d, 0, 128:256, :])
            p1 = dot_nn(v_e, qt[d, 1, 128:256, :])
            s2 = dot_nn(k_cat, qt[d, 0])
            p2 = dot_nn(v_cat, qt[d, 1])
            st.append((d, low_rows, high_rows, low_wide, k_cat, s1, p1, s2, p2, q_e, q_l, g_e, g_l))
        tot = None
        for (d, low_rows, high_rows, low_wide, k_cat, s1, p1, s2, p2, q_e, q_l, g_e, g_l) in st:
            lse_e, lse_l = meta[d, 0:1, 0:ROWS], meta[d, 0:1, ROWS : 2 * ROWS]
            del_e, del_l = meta[d, 1:2, 0:ROWS], meta[d, 1:2, ROWS : 2 * ROWS]
            probs = probs_of(s1, lse_l)
            grad_scores = (probs * (p1 - del_l)).astype(BF16)
            dv_e = dot_nn(probs.astype(BF16), g_l)
            dk_e = dot_nn(grad_scores, q_l)
            dq_l = dot_tn(k_e, grad_scores)
            q_cat = jnp.concatenate([q_e, q_l], axis=1)
            g_cat = jnp.concatenate([g_e, g_l], axis=1)
            lse = jnp.where(low_wide > 0.5, lse_e[None], lse_l[None])
            delta = jnp.where(low_wide > 0.5, del_e[None], del_l[None])
            scores = s2.reshape(SIDE, SPAN, ROWS) * (SCALE * LOG2E) - lse
            row_k = lax.broadcasted_iota(jnp.int32, (SPAN, ROWS), 0)
            col_r = lax.broadcasted_iota(jnp.int32, (SPAN, ROWS), 1) // GROUP
            seen = row_k <= col_r + jnp.where(own, 0, SPAN)
            first = jnp.where(seen, scores[0], -1e30)
            scores = jnp.concatenate([first[None], scores[1:]], axis=0)
            probs = jnp.exp2(scores)
            grad_probs = p2.reshape(SIDE, SPAN, ROWS)
            grad_scores = (probs * (grad_probs - delta)).astype(BF16).reshape(KEYS, ROWS)
            probs = probs.astype(BF16).reshape(KEYS, ROWS)
            dv = dot_nn(probs, g_cat)
            dk = dot_nn(grad_scores, q_cat)
            dq = dot_tn(k_cat, grad_scores)
            dqt[d, 0:128, :] += dq[0:128]
            dqt[d, 128:256, :] += dq[128:256] + dq_l
            parts = [dk_e + dk[:, 0:128] * low_rows, dk[:, 128:256] * high_rows, dv_e + dv[:, 0:128] * low_rows, dv[:, 128:256] * high_rows]
            tot = parts if tot is None else [x + y for x, y in zip(tot, parts)]
            own = False
        for n in range(4):
            acc[slots, SPAN * n : SPAN * (n + 1), :] += tot[n].reshape(SIDE, SPAN, DIM)

    def send_y(c):
        for n in range(1, SIDE):
            part[c, n - 1] = acc[SIDE * c + n].astype(BF16)
            ry_go[c][n - 1].start()

    def sum_y(c):
        arrive(ry_go[c])
        total = acc[SIDE * c]
        for n in range(SIDE - 1):
            total = total + ybuf[c, n].astype(F32)
        return total

    def send_z(c):
        zpart[c - 1] = sum_y(c).astype(BF16)
        rz_go[c].start()

    def send_x(d):
        xpart[d - 1] = dqt[d].astype(BF16)
        rx_go[d].start()

    def pick(i, table):
        value = jnp.int32(table[-1])
        for n, entry in enumerate(table[:-1]):
            value = jnp.where(i == n, entry, value)
        return value

    def finish_x():
        arrive(rx_go[1:])
        total = dqt[0]
        for n in range(SIDE - 1):
            total = total + xbuf[n].astype(F32)
        total = total * SCALE
        out[0:ROWS, :] = total[0:128].T.astype(BF16)
        out[ROWS : 2 * ROWS, :] = total[128:256].T.astype(BF16)

    def finish_kv():
        own = sum_y(0)
        arrive(rz_go[1:])
        for n in range(SIDE - 1):
            own = own + zbuf[n].astype(F32)
        out[512:640, :] = (own[0:128] * SCALE).astype(BF16)
        out[640:768, :] = own[128:256].astype(BF16)

    def need_q(d):
        arrive(q_go[d] + [meta_go[d]])
        turn(d)

    actions = {
        "need_y": lambda c: arrive(y_go[c]),
        "need_q": need_q,
        "send_y": send_y,
        "send_z": send_z,
        "send_x": send_x,
    }

    def act(names):
        for name in names:
            actions[name[:-1]](int(name[-1]))

    def loop_step(i, carry):
        for n in BEFORE:
            pl.when(i == n)(lambda n=n: act(BEFORE[n]))
        c = pick(i, [entry[1] for entry in ORDER])
        for group in GROUPS:
            chosen = pick(i, [int(entry[0] == group) for entry in ORDER])
            pl.when(chosen == 1)(lambda group=group: step(GROUPS[group], c, i == 0))
        for n in AFTER:
            pl.when(i == n)(lambda n=n: act(AFTER[n]))
        return carry

    turn(0)
    arrive(y_go[0])
    own_early()
    lax.fori_loop(0, len(ORDER), loop_step, 0)
    act(LAST)
    finish_x()
    finish_kv()
    for copy in links.made:
        copy.wait_send()


COPIES = 9 + 3 + 12 + 12 + 3 + 3
GROUPS = {"t": (0, 1, 3), "s": (2,)}
ORDER = (("t", 0), ("t", 1), ("t", 3), ("s", 1), ("s", 3), ("t", 2), ("s", 2), ("s", 0))
BEFORE = {0: ("need_q1", "need_q3"), 1: ("need_y1",), 2: ("need_y3",), 3: ("need_q2",), 5: ("need_y2",)}
AFTER = {3: ("send_y1",), 4: ("send_y3",), 5: ("send_x1", "send_x3"), 6: ("send_y2", "send_z1")}
LAST = ("send_x2", "send_y0", "send_z3", "send_z2")


def body(queries, keys, values, grad_out, saved_stats, positions):
    hbm_spec = pl.BlockSpec(memory_space=pltpu.HBM)
    vmem_spec = pl.BlockSpec(memory_space=pltpu.VMEM)
    grads = pl.pallas_call(
        kernel,
        out_shape=jax.ShapeDtypeStruct((768, DIM), BF16),
        in_specs=[hbm_spec] * 6,
        out_specs=vmem_spec,
        scratch_shapes=[
            pltpu.VMEM((4, 2, 512, DIM), BF16),
            pltpu.VMEM((16, 272, DIM), BF16),
            pltpu.VMEM((4, 8, 512), F32),
            pltpu.VMEM((8, 128), F32),
            pltpu.VMEM((1, 128), jnp.int32),
            pltpu.VMEM((4, 2, 256, ROWS), BF16),
            pltpu.VMEM((16, 256, DIM), F32),
            pltpu.VMEM((4, 256, ROWS), F32),
            pltpu.VMEM((4, 3, 256, DIM), BF16),
            pltpu.VMEM((4, 3, 256, DIM), BF16),
            pltpu.VMEM((3, 256, DIM), BF16),
            pltpu.VMEM((3, 256, DIM), BF16),
            pltpu.VMEM((3, 256, ROWS), BF16),
            pltpu.VMEM((3, 256, ROWS), BF16),
            pltpu.SemaphoreType.DMA((7,)),
            pltpu.SemaphoreType.DMA((COPIES,)),
            pltpu.SemaphoreType.DMA((COPIES,)),
        ],
        compiler_params=pltpu.CompilerParams(
            collective_id=0, has_side_effects=True, vmem_limit_bytes=62 * 1024 * 1024
        ),
    )(
        queries.reshape(512, DIM),
        keys.reshape(128, DIM),
        values.reshape(128, DIM),
        grad_out.reshape(512, DIM),
        saved_stats.reshape(8, 128),
        positions.reshape(1, 128),
    )
    return (
        grads[0:512].reshape(128, GROUP, DIM),
        grads[512:640].reshape(128, 1, DIM),
        grads[640:768].reshape(128, 1, DIM),
    )


def solution(mesh):
    in_specs = (
        P("ctx", "tp", None),
        P("ctx", "tp", None),
        P("ctx", "tp", None),
        P("ctx", "tp", None),
        P(None, "tp", "ctx"),
        P("ctx"),
    )
    out_specs = (P("ctx", "tp", None), P("ctx", "tp", None), P("ctx", "tp", None))
    return jax.shard_map(body, mesh=mesh, in_specs=in_specs, out_specs=out_specs, check_vma=False)
```

```python
import math

import jax
import jax.numpy as jnp
from jax import lax
from jax.experimental import pallas as pl
from jax.experimental.pallas import tpu as pltpu
from jax.sharding import PartitionSpec as P

SIDE = 4
SPAN = 64
DIM = 128
GROUP = 4
ROWS = SPAN * GROUP
KEYS = SPAN * SIDE
LOG2E = 1.4426950408889634
SCALE = 1.0 / math.sqrt(DIM)
F32 = jnp.float32
BF16 = jnp.bfloat16
MESH = pl.DeviceIdType.MESH


def dot_nt(a, b):
    return lax.dot_general(a, b, (((1,), (1,)), ((), ())), preferred_element_type=F32)


def dot_tn(a, b):
    return lax.dot_general(a, b, (((0,), (0,)), ((), ())), preferred_element_type=F32)


def dot_nn(a, b):
    return jnp.dot(a, b, preferred_element_type=F32)


class Links:
    def __init__(self, send_sems, recv_sems):
        self.send_sems = send_sems
        self.recv_sems = recv_sems
        self.count = 0
        self.made = []

    def copy(self, src, dst, device):
        made = pltpu.make_async_remote_copy(
            src_ref=src,
            dst_ref=dst,
            send_sem=self.send_sems.at[self.count],
            recv_sem=self.recv_sems.at[self.count],
            device_id={"ctx": device},
            device_id_type=MESH,
        )
        self.count += 1
        self.made.append(made)
        return made


def kernel(
    q_in, k_in, v_in, g_in, st_in, pos_in,
    out,
    qd, kv, meta, stats, pos, qt, acc, dqt,
    part, ybuf, zpart, zbuf, lpart, lbuf, xpart, xbuf,
    local_sems, send_sems, recv_sems,
):
    me = lax.axis_index("ctx")
    z, x, y = me // (SIDE * SIDE), (me // SIDE) % SIDE, me % SIDE

    def at(dz=0, dx=0, dy=0):
        return (
            ((z + dz) % SIDE) * (SIDE * SIDE) + ((x + dx) % SIDE) * SIDE + (y + dy) % SIDE
        )

    peers = [at(dx=1), at(dx=2), at(dx=3), at(dy=1), at(dy=2), at(dy=3), at(dz=1), at(dz=2), at(dz=3)]

    loads = [
        pltpu.make_async_copy(q_in, qd.at[0, 0], local_sems.at[0]),
        pltpu.make_async_copy(g_in, qd.at[0, 1], local_sems.at[1]),
        pltpu.make_async_copy(k_in, kv.at[0, pl.ds(0, 128)], local_sems.at[2]),
        pltpu.make_async_copy(v_in.at[pl.ds(0, 64)], kv.at[0, pl.ds(128, 64)], local_sems.at[3]),
        pltpu.make_async_copy(v_in.at[pl.ds(64, 64)], kv.at[0, pl.ds(208, 64)], local_sems.at[6]),
        pltpu.make_async_copy(st_in, stats, local_sems.at[4]),
        pltpu.make_async_copy(pos_in, pos, local_sems.at[5]),
    ]
    for load in loads:
        load.start()
    barrier = pltpu.get_barrier_semaphore()
    for peer in peers:
        pl.semaphore_signal(barrier, inc=1, device_id={"ctx": peer}, device_id_type=MESH)

    for load in loads[2:5] + loads[6:]:
        load.wait()
    span = (pos[0:1, 0:1] // SPAN).astype(F32)
    kv[0, 192:208, :] = jnp.broadcast_to(span, (16, DIM)).astype(BF16)

    links = Links(send_sems, recv_sems)
    head, tail = pl.ds(0, 208), pl.ds(208, 64)
    z_head = [None] + [
        links.copy(kv.at[0, head], kv.at[SIDE * s, head], at(dz=SIDE - s)) for s in range(1, SIDE)
    ]
    z_tail = [None] + [
        [
            links.copy(kv.at[n, tail], kv.at[SIDE * s + n, tail], at(dz=SIDE - s))
            for s in range(1, SIDE)
        ]
        for n in range(1, SIDE)
    ]
    z_tail[0] = [
        links.copy(kv.at[0, tail], kv.at[SIDE * s, tail], at(dz=SIDE - s)) for s in range(1, SIDE)
    ]
    y_tail = [None] + [
        links.copy(kv.at[0, tail], kv.at[s, tail], at(dy=SIDE - s)) for s in range(1, SIDE)
    ]
    y_head = [
        [
            links.copy(kv.at[SIDE * c, head], kv.at[SIDE * c + s, head], at(dy=SIDE - s))
            for s in range(1, SIDE)
        ]
        for c in range(SIDE)
    ]
    halves = (pl.ds(0, ROWS), pl.ds(ROWS, ROWS))
    q_right = [
        [links.copy(qd.at[0, n, h], qd.at[3, n, h], at(dx=1)) for h in halves] for n in range(2)
    ]
    q_left = [
        [links.copy(qd.at[0, n, h], qd.at[1, n, h], at(dx=3)) for h in halves] for n in range(2)
    ]
    on_right = [links.copy(qd.at[3, 0, h], qd.at[2, 0, h], at(dx=1)) for h in halves]
    on_left = [links.copy(qd.at[1, 1, h], qd.at[2, 1, h], at(dx=3)) for h in halves]
    meta_go = [None] + [
        links.copy(meta.at[0], meta.at[s], at(dx=SIDE - s)) for s in range(1, SIDE)
    ]
    q_come = [None, q_left[0], on_right + on_left, q_right[1]]
    most, last = pl.ds(0, 192), pl.ds(192, 64)
    ry_most = [
        [
            links.copy(part.at[c, s - 1, most], ybuf.at[c, s - 1, most], at(dy=s))
            for s in range(1, SIDE)
        ]
        for c in range(SIDE)
    ]
    ry_last = [
        links.copy(part.at[0, s - 1, last], ybuf.at[0, s - 1, last], at(dy=s))
        for s in range(1, SIDE)
    ]
    rz_most = [None] + [
        links.copy(zpart.at[s - 1], zbuf.at[s - 1], at(dz=s)) for s in range(1, SIDE)
    ]
    rz_last = [None] + [
        links.copy(lpart.at[s - 1], lbuf.at[s - 1], at(dz=s)) for s in range(1, SIDE)
    ]
    rx_go = [None] + [
        links.copy(xpart.at[s - 1], xbuf.at[s - 1], at(dx=s)) for s in range(1, SIDE)
    ]

    def start(copies):
        for copy in copies:
            copy.start()

    def arrive(copies):
        for copy in copies:
            copy.wait_recv()

    pl.semaphore_wait(barrier, len(peers))
    start((z_head[1], z_head[3], z_head[2]))
    start(y_tail[1:])
    start(y_head[0])
    start(z_tail[0])
    for load in loads[0:2]:
        load.wait()
    for h in range(2):
        start((q_right[0][h], q_left[1][h]))
    for h in range(2):
        start((q_right[1][h], q_left[0][h]))

    loads[5].wait()
    spread_t = lax.broadcasted_iota(jnp.int32, (128, 512), 0)
    spread_r = lax.broadcasted_iota(jnp.int32, (128, 512), 1)
    spread = jnp.where(spread_r // GROUP == spread_t, 1.0, 0.0).astype(F32)
    wide = jnp.dot(
        stats[...], spread, preferred_element_type=F32, precision=lax.Precision.HIGHEST
    )
    head_of = lax.broadcasted_iota(jnp.int32, (8, 512), 0) % GROUP
    lane_of = lax.broadcasted_iota(jnp.int32, (8, 512), 1) % GROUP
    wide = jnp.where(head_of == lane_of, wide, 0.0)
    meta[0, 0:1, :] = jnp.sum(wide[0:4], axis=0, keepdims=True) * LOG2E
    meta[0, 1:2, :] = jnp.sum(wide[4:8], axis=0, keepdims=True)
    meta[0, 2:3, :] = jnp.broadcast_to(span, (1, 512))
    meta[0, 3:8, :] = jnp.zeros((5, 512), F32)
    start(meta_go[1:])

    def forward_q(h):
        arrive([q_right[0][h]])
        start([on_right[h]])
        arrive([q_left[1][h]])
        start([on_left[h]])

    def forward_z(c):
        arrive([z_head[c]])
        start(y_head[c])

    def forward_y(n):
        arrive([y_tail[n]])
        start(z_tail[n])

    forward_z(1)
    forward_q(0)
    forward_z(3)
    forward_y(1)
    forward_y(3)
    forward_q(1)
    forward_z(2)
    forward_y(2)

    acc[...] = jnp.zeros_like(acc)
    dqt[...] = jnp.zeros_like(dqt)

    def probs_of(scores, log_total):
        return jnp.exp2(scores * (SCALE * LOG2E) - log_total)

    def turn(d):
        for n in range(2):
            qt[d, n, 0:128, :] = qd[d, n, 0:ROWS, :].T
            qt[d, n, 128:256, :] = qd[d, n, ROWS : 2 * ROWS, :].T

    def own_early():
        key, value = kv[0, 0:64, :], kv[0, 128:192, :]
        query, grad = qd[0, 0, 0:ROWS, :], qd[0, 1, 0:ROWS, :]
        row_k = lax.broadcasted_iota(jnp.int32, (SPAN, ROWS), 0)
        col_r = lax.broadcasted_iota(jnp.int32, (SPAN, ROWS), 1) // GROUP
        scores = dot_nt(key, query) * (SCALE * LOG2E) - meta[0, 0:1, 0:ROWS]
        probs = jnp.exp2(jnp.where(row_k <= col_r, scores, -1e30))
        grad_probs = dot_nt(value, grad)
        grad_scores = (probs * (grad_probs - meta[0, 1:2, 0:ROWS])).astype(BF16)
        acc[0, 128:192, :] += dot_nn(probs.astype(BF16), grad)
        acc[0, 0:64, :] += dot_nn(grad_scores, query)
        dqt[0, 0:128, :] += dot_tn(key, grad_scores)

    def step(group, c, own):
        base = SIDE * c
        slots = pl.ds(base, SIDE)

        def rows(start):
            return kv[slots, start : start + SPAN, :].reshape(KEYS, DIM)

        k_e, k_l, v_e, v_l = rows(0), rows(64), rows(128), rows(208)
        span_k = kv[slots, 192:208, :].astype(F32)[:, 0:1, :]
        st = []
        for d in group:
            q_e, q_l = qd[d, 0, 0:ROWS, :], qd[d, 0, ROWS : 2 * ROWS, :]
            g_e, g_l = qd[d, 1, 0:ROWS, :], qd[d, 1, ROWS : 2 * ROWS, :]
            span_q = meta[d, 2:3, 0:DIM]
            low = jnp.where(span_k < span_q[None], 1.0, 0.0)
            low_rows = jnp.broadcast_to(low, (SIDE, SPAN, DIM)).reshape(KEYS, DIM)
            high_rows = 1.0 - low_rows
            low_wide = jnp.concatenate([low, low], axis=2)
            low_b, high_b = low_rows.astype(BF16), high_rows.astype(BF16)
            k_cat = jnp.concatenate([k_e * low_b, k_l * high_b], axis=1)
            v_cat = jnp.concatenate([v_e * low_b, v_l * high_b], axis=1)
            s1 = dot_nn(k_e, qt[d, 0, 128:256, :])
            p1 = dot_nn(v_e, qt[d, 1, 128:256, :])
            s2 = dot_nn(k_cat, qt[d, 0])
            p2 = dot_nn(v_cat, qt[d, 1])
            st.append((d, low_rows, high_rows, low_wide, k_cat, s1, p1, s2, p2, q_e, q_l, g_e, g_l))
        tot = None
        for (d, low_rows, high_rows, low_wide, k_cat, s1, p1, s2, p2, q_e, q_l, g_e, g_l) in st:
            lse_e, lse_l = meta[d, 0:1, 0:ROWS], meta[d, 0:1, ROWS : 2 * ROWS]
            del_e, del_l = meta[d, 1:2, 0:ROWS], meta[d, 1:2, ROWS : 2 * ROWS]
            probs = probs_of(s1, lse_l)
            grad_scores = (probs * (p1 - del_l)).astype(BF16)
            dv_e = dot_nn(probs.astype(BF16), g_l)
            dk_e = dot_nn(grad_scores, q_l)
            dq_l = dot_tn(k_e, grad_scores)
            q_cat = jnp.concatenate([q_e, q_l], axis=1)
            g_cat = jnp.concatenate([g_e, g_l], axis=1)
            lse = jnp.where(low_wide > 0.5, lse_e[None], lse_l[None])
            delta = jnp.where(low_wide > 0.5, del_e[None], del_l[None])
            scores = s2.reshape(SIDE, SPAN, ROWS) * (SCALE * LOG2E) - lse
            row_k = lax.broadcasted_iota(jnp.int32, (SPAN, ROWS), 0)
            col_r = lax.broadcasted_iota(jnp.int32, (SPAN, ROWS), 1) // GROUP
            seen = row_k <= col_r + jnp.where(own, 0, SPAN)
            first = jnp.where(seen, scores[0], -1e30)
            scores = jnp.concatenate([first[None], scores[1:]], axis=0)
            probs = jnp.exp2(scores)
            grad_probs = p2.reshape(SIDE, SPAN, ROWS)
            grad_scores = (probs * (grad_probs - delta)).astype(BF16).reshape(KEYS, ROWS)
            probs = probs.astype(BF16).reshape(KEYS, ROWS)
            dv = dot_nn(probs, g_cat)
            dk = dot_nn(grad_scores, q_cat)
            dq = dot_tn(k_cat, grad_scores)
            dqt[d, 0:128, :] += dq[0:128]
            dqt[d, 128:256, :] += dq[128:256] + dq_l
            parts = [dk_e + dk[:, 0:128] * low_rows, dk[:, 128:256] * high_rows, dv_e + dv[:, 0:128] * low_rows, dv[:, 128:256] * high_rows]
            tot = parts if tot is None else [x + y for x, y in zip(tot, parts)]
            own = False
        for n in range(4):
            acc[slots, SPAN * n : SPAN * (n + 1), :] += tot[n].reshape(SIDE, SPAN, DIM)

    def send_y(c):
        for n in range(1, SIDE):
            part[c, n - 1, 0:192] = acc[SIDE * c + n, 0:192].astype(BF16)
            ry_most[c][n - 1].start()
        if c:
            lpart[c - 1] = acc[SIDE * c : SIDE * (c + 1), 192:256].astype(BF16)
            rz_last[c].start()

    def sum_y(c):
        arrive(ry_most[c])
        total = acc[SIDE * c, 0:192]
        for n in range(SIDE - 1):
            total = total + ybuf[c, n, 0:192].astype(F32)
        return total

    def send_z(c):
        zpart[c - 1] = sum_y(c).astype(BF16)
        rz_most[c].start()

    def turn_last():
        arrive(rz_last[1:])
        for n in (2, 1, 3, 0):
            total = acc[n, 192:256]
            for s in range(SIDE - 1):
                total = total + lbuf[s, n].astype(F32)
            if n:
                part[0, n - 1, 192:256] = total.astype(BF16)
                ry_last[n - 1].start()
            else:
                acc[0, 192:256] = total

    def send_x(d):
        xpart[d - 1] = dqt[d].astype(BF16)
        rx_go[d].start()

    def pick(i, table):
        value = jnp.int32(table[-1])
        for n, entry in enumerate(table[:-1]):
            value = jnp.where(i == n, entry, value)
        return value

    def finish_x():
        arrive(rx_go[1:])
        total = dqt[0]
        for n in range(SIDE - 1):
            total = total + xbuf[n].astype(F32)
        total = total * SCALE
        out[0:ROWS, :] = total[0:128].T.astype(BF16)
        out[ROWS : 2 * ROWS, :] = total[128:256].T.astype(BF16)

    def finish_kv():
        most_sum = sum_y(0)
        arrive(rz_most[1:])
        for n in range(SIDE - 1):
            most_sum = most_sum + zbuf[n].astype(F32)
        out[512:640, :] = (most_sum[0:128] * SCALE).astype(BF16)
        out[640:704, :] = most_sum[128:192].astype(BF16)
        arrive(ry_last)
        last_sum = acc[0, 192:256]
        for n in range(SIDE - 1):
            last_sum = last_sum + ybuf[0, n, 192:256].astype(F32)
        out[704:768, :] = last_sum.astype(BF16)

    def need_y(c):
        arrive(y_head[c])
        if c:
            arrive([z_tail[n][c - 1] for n in range(SIDE)])

    def need_q(d):
        arrive(q_come[d] + [meta_go[d]])
        turn(d)

    actions = {
        "need_y": need_y,
        "need_q": need_q,
        "send_y": send_y,
        "send_z": send_z,
        "send_x": send_x,
        "turn_last": lambda unused: turn_last(),
    }

    def act(names):
        for name in names:
            actions[name[:-1]](int(name[-1]))

    def loop_step(i, carry):
        for n in BEFORE:
            pl.when(i == n)(lambda n=n: act(BEFORE[n]))
        c = pick(i, [entry[1] for entry in ORDER])
        for group in GROUPS:
            chosen = pick(i, [int(entry[0] == group) for entry in ORDER])
            pl.when(chosen == 1)(lambda group=group: step(GROUPS[group], c, i == 0))
        for n in AFTER:
            pl.when(i == n)(lambda n=n: act(AFTER[n]))
        return carry

    turn(0)
    need_y(0)
    own_early()
    lax.fori_loop(0, len(ORDER), loop_step, 0)
    act(LAST)
    finish_x()
    finish_kv()
    for copy in links.made:
        copy.wait_send()


COPIES = 3 + 12 + 3 + 12 + 8 + 4 + 3 + 12 + 3 + 3 + 3 + 3
GROUPS = {"t": (0, 1, 3), "s": (2,)}
ORDER = (("t", 0), ("t", 1), ("t", 3), ("s", 1), ("s", 3), ("t", 2), ("s", 2), ("s", 0))
BEFORE = {0: ("need_q1", "need_q3"), 1: ("need_y1",), 2: ("need_y3",), 3: ("need_q2",), 5: ("need_y2",)}
AFTER = {3: ("send_y1",), 4: ("send_y3",), 5: ("send_x1", "send_x3"), 6: ("send_y2", "send_z1")}
LAST = ("send_x2", "send_y0", "send_z3", "turn_last0", "send_z2")


def body(queries, keys, values, grad_out, saved_stats, positions):
    hbm_spec = pl.BlockSpec(memory_space=pltpu.HBM)
    vmem_spec = pl.BlockSpec(memory_space=pltpu.VMEM)
    grads = pl.pallas_call(
        kernel,
        out_shape=jax.ShapeDtypeStruct((768, DIM), BF16),
        in_specs=[hbm_spec] * 6,
        out_specs=vmem_spec,
        scratch_shapes=[
            pltpu.VMEM((4, 2, 512, DIM), BF16),
            pltpu.VMEM((16, 272, DIM), BF16),
            pltpu.VMEM((4, 8, 512), F32),
            pltpu.VMEM((8, 128), F32),
            pltpu.VMEM((1, 128), jnp.int32),
            pltpu.VMEM((4, 2, 256, ROWS), BF16),
            pltpu.VMEM((16, 256, DIM), F32),
            pltpu.VMEM((4, 256, ROWS), F32),
            pltpu.VMEM((4, 3, 256, DIM), BF16),
            pltpu.VMEM((4, 3, 256, DIM), BF16),
            pltpu.VMEM((3, 192, DIM), BF16),
            pltpu.VMEM((3, 192, DIM), BF16),
            pltpu.VMEM((3, 4, 64, DIM), BF16),
            pltpu.VMEM((3, 4, 64, DIM), BF16),
            pltpu.VMEM((3, 256, ROWS), BF16),
            pltpu.VMEM((3, 256, ROWS), BF16),
            pltpu.SemaphoreType.DMA((7,)),
            pltpu.SemaphoreType.DMA((COPIES,)),
            pltpu.SemaphoreType.DMA((COPIES,)),
        ],
        compiler_params=pltpu.CompilerParams(
            collective_id=0, has_side_effects=True, vmem_limit_bytes=62 * 1024 * 1024
        ),
    )(
        queries.reshape(512, DIM),
        keys.reshape(128, DIM),
        values.reshape(128, DIM),
        grad_out.reshape(512, DIM),
        saved_stats.reshape(8, 128),
        positions.reshape(1, 128),
    )
    return (
        grads[0:512].reshape(128, GROUP, DIM),
        grads[512:640].reshape(128, 1, DIM),
        grads[640:768].reshape(128, 1, DIM),
    )


def solution(mesh):
    in_specs = (
        P("ctx", "tp", None),
        P("ctx", "tp", None),
        P("ctx", "tp", None),
        P("ctx", "tp", None),
        P(None, "tp", "ctx"),
        P("ctx"),
    )
    out_specs = (P("ctx", "tp", None), P("ctx", "tp", None), P("ctx", "tp", None))
    return jax.shard_map(body, mesh=mesh, in_specs=in_specs, out_specs=out_specs, check_vma=False)
```

```python
import math

import jax
import jax.numpy as jnp
from jax import lax
from jax.experimental import pallas as pl
from jax.experimental.pallas import tpu as pltpu
from jax.sharding import PartitionSpec as P

SIDE = 4
SPAN = 64
DIM = 128
GROUP = 4
ROWS = SPAN * GROUP
KEYS = SPAN * SIDE
LOG2E = 1.4426950408889634
SCALE = 1.0 / math.sqrt(DIM)
F32 = jnp.float32
BF16 = jnp.bfloat16
MESH = pl.DeviceIdType.MESH


def dot_nt(a, b):
    return lax.dot_general(a, b, (((1,), (1,)), ((), ())), preferred_element_type=F32)


def dot_tn(a, b):
    return lax.dot_general(a, b, (((0,), (0,)), ((), ())), preferred_element_type=F32)


def dot_nn(a, b):
    return jnp.dot(a, b, preferred_element_type=F32)


class Links:
    def __init__(self, send_sems, recv_sems):
        self.send_sems = send_sems
        self.recv_sems = recv_sems
        self.count = 0
        self.made = []

    def copy(self, src, dst, device):
        made = pltpu.make_async_remote_copy(
            src_ref=src,
            dst_ref=dst,
            send_sem=self.send_sems.at[self.count],
            recv_sem=self.recv_sems.at[self.count],
            device_id={"ctx": device},
            device_id_type=MESH,
        )
        self.count += 1
        self.made.append(made)
        return made


def kernel(
    q_in, k_in, v_in, g_in, st_in, pos_in,
    out,
    qd, kv, meta, stats, pos, qt, acc, dqt,
    part, ybuf, zpart, zbuf, lpart, lbuf, xpart, xbuf,
    local_sems, send_sems, recv_sems,
):
    me = lax.axis_index("ctx")
    z, x, y = me // (SIDE * SIDE), (me // SIDE) % SIDE, me % SIDE

    def at(dz=0, dx=0, dy=0):
        return (
            ((z + dz) % SIDE) * (SIDE * SIDE) + ((x + dx) % SIDE) * SIDE + (y + dy) % SIDE
        )

    peers = [at(dx=1), at(dx=2), at(dx=3), at(dy=1), at(dy=2), at(dy=3), at(dz=1), at(dz=2), at(dz=3)]

    loads = [
        pltpu.make_async_copy(q_in, qd.at[0, 0], local_sems.at[0]),
        pltpu.make_async_copy(g_in, qd.at[0, 1], local_sems.at[1]),
        pltpu.make_async_copy(k_in, kv.at[0, pl.ds(0, 128)], local_sems.at[2]),
        pltpu.make_async_copy(v_in.at[pl.ds(0, 64)], kv.at[0, pl.ds(128, 64)], local_sems.at[3]),
        pltpu.make_async_copy(v_in.at[pl.ds(64, 64)], kv.at[0, pl.ds(208, 64)], local_sems.at[6]),
        pltpu.make_async_copy(st_in, stats, local_sems.at[4]),
        pltpu.make_async_copy(pos_in, pos, local_sems.at[5]),
    ]
    for load in loads:
        load.start()
    barrier = pltpu.get_barrier_semaphore()
    for peer in peers:
        pl.semaphore_signal(barrier, inc=1, device_id={"ctx": peer}, device_id_type=MESH)

    for load in loads[2:5] + loads[6:]:
        load.wait()
    span = (pos[0:1, 0:1] // SPAN).astype(F32)
    kv[0, 192:208, :] = jnp.broadcast_to(span, (16, DIM)).astype(BF16)

    links = Links(send_sems, recv_sems)
    head, tail = pl.ds(0, 208), pl.ds(208, 64)
    z_head = [None] + [
        links.copy(kv.at[0, head], kv.at[SIDE * s, head], at(dz=SIDE - s)) for s in range(1, SIDE)
    ]
    z_tail = [None] + [
        [
            links.copy(kv.at[n, tail], kv.at[SIDE * s + n, tail], at(dz=SIDE - s))
            for s in range(1, SIDE)
        ]
        for n in range(1, SIDE)
    ]
    z_tail[0] = [
        links.copy(kv.at[0, tail], kv.at[SIDE * s, tail], at(dz=SIDE - s)) for s in range(1, SIDE)
    ]
    y_tail = [None] + [
        links.copy(kv.at[0, tail], kv.at[s, tail], at(dy=SIDE - s)) for s in range(1, SIDE)
    ]
    y_head = [
        [
            links.copy(kv.at[SIDE * c, head], kv.at[SIDE * c + s, head], at(dy=SIDE - s))
            for s in range(1, SIDE)
        ]
        for c in range(SIDE)
    ]
    halves = (pl.ds(0, ROWS), pl.ds(ROWS, ROWS))
    q_right = [
        [links.copy(qd.at[0, n, h], qd.at[3, n, h], at(dx=1)) for h in halves] for n in range(2)
    ]
    q_left = [
        [links.copy(qd.at[0, n, h], qd.at[1, n, h], at(dx=3)) for h in halves] for n in range(2)
    ]
    on_right = [links.copy(qd.at[3, 0, h], qd.at[2, 0, h], at(dx=1)) for h in halves]
    on_left = [links.copy(qd.at[1, 1, h], qd.at[2, 1, h], at(dx=3)) for h in halves]
    meta_go = [None] + [
        links.copy(meta.at[0], meta.at[s], at(dx=SIDE - s)) for s in range(1, SIDE)
    ]
    q_come = [None, q_left[0], on_right + on_left, q_right[1]]
    most, last = pl.ds(0, 192), pl.ds(192, 64)
    ry_most = [
        [
            links.copy(part.at[c, s - 1, most], ybuf.at[c, s - 1, most], at(dy=s))
            for s in range(1, SIDE)
        ]
        for c in range(SIDE)
    ]
    ry_last = [
        links.copy(part.at[0, s - 1, last], ybuf.at[0, s - 1, last], at(dy=s))
        for s in range(1, SIDE)
    ]
    rz_most = [None] + [
        links.copy(zpart.at[s - 1], zbuf.at[s - 1], at(dz=s)) for s in range(1, SIDE)
    ]
    rz_last = [None] + [
        links.copy(lpart.at[s - 1], lbuf.at[s - 1], at(dz=s)) for s in range(1, SIDE)
    ]
    rx_go = [None] + [
        links.copy(xpart.at[s - 1], xbuf.at[s - 1], at(dx=s)) for s in range(1, SIDE)
    ]

    def start(copies):
        for copy in copies:
            copy.start()

    def sent(copies):
        for copy in copies:
            copy.wait_send()

    def arrive(copies):
        for copy in copies:
            copy.wait_recv()

    pl.semaphore_wait(barrier, len(peers))
    start((z_head[1], z_head[3]))
    start(y_tail[1:])
    start(y_head[0])
    for load in loads[0:2]:
        load.wait()
    for h in range(2):
        start((q_right[0][h], q_left[1][h]))
    for h in range(2):
        start((q_right[1][h], q_left[0][h]))

    loads[5].wait()
    spread_t = lax.broadcasted_iota(jnp.int32, (128, 512), 0)
    spread_r = lax.broadcasted_iota(jnp.int32, (128, 512), 1)
    spread = jnp.where(spread_r // GROUP == spread_t, 1.0, 0.0).astype(F32)
    wide = jnp.dot(
        stats[...], spread, preferred_element_type=F32, precision=lax.Precision.HIGHEST
    )
    head_of = lax.broadcasted_iota(jnp.int32, (8, 512), 0) % GROUP
    lane_of = lax.broadcasted_iota(jnp.int32, (8, 512), 1) % GROUP
    wide = jnp.where(head_of == lane_of, wide, 0.0)
    meta[0, 0:1, :] = jnp.sum(wide[0:4], axis=0, keepdims=True) * LOG2E
    meta[0, 1:2, :] = jnp.sum(wide[4:8], axis=0, keepdims=True)
    meta[0, 2:3, :] = jnp.broadcast_to(span, (1, 512))
    meta[0, 3:8, :] = jnp.zeros((5, 512), F32)
    start(meta_go[1:])

    def forward_q(h):
        arrive([q_right[0][h]])
        start([on_right[h]])
        arrive([q_left[1][h]])
        start([on_left[h]])

    def forward_z(c):
        arrive([z_head[c]])
        start(y_head[c])

    def forward_y(n):
        arrive([y_tail[n]])
        start(z_tail[n])

    forward_z(1)
    start([z_head[2]])
    forward_z(3)
    start(z_tail[0])
    forward_y(1)
    forward_y(3)
    forward_y(2)
    forward_z(2)
    forward_q(0)
    forward_q(1)

    acc[...] = jnp.zeros_like(acc)
    dqt[...] = jnp.zeros_like(dqt)

    def probs_of(scores, log_total):
        return jnp.exp2(scores * (SCALE * LOG2E) - log_total)

    def turn(d):
        for n in range(2):
            qt[d, n, 0:128, :] = qd[d, n, 0:ROWS, :].T
            qt[d, n, 128:256, :] = qd[d, n, ROWS : 2 * ROWS, :].T

    def own_early():
        key, value = kv[0, 0:64, :], kv[0, 128:192, :]
        query, grad = qd[0, 0, 0:ROWS, :], qd[0, 1, 0:ROWS, :]
        row_k = lax.broadcasted_iota(jnp.int32, (SPAN, ROWS), 0)
        col_r = lax.broadcasted_iota(jnp.int32, (SPAN, ROWS), 1) // GROUP
        scores = dot_nt(key, query) * (SCALE * LOG2E) - meta[0, 0:1, 0:ROWS]
        probs = jnp.exp2(jnp.where(row_k <= col_r, scores, -1e30))
        grad_probs = dot_nt(value, grad)
        grad_scores = (probs * (grad_probs - meta[0, 1:2, 0:ROWS])).astype(BF16)
        acc[0, 128:192, :] += dot_nn(probs.astype(BF16), grad)
        acc[0, 0:64, :] += dot_nn(grad_scores, query)
        dqt[0, 0:128, :] += dot_tn(key, grad_scores)

    def step(group, c, own):
        base = SIDE * c
        slots = pl.ds(base, SIDE)

        def rows(start):
            return kv[slots, start : start + SPAN, :].reshape(KEYS, DIM)

        k_e, k_l, v_e, v_l = rows(0), rows(64), rows(128), rows(208)
        span_k = kv[slots, 192:208, :].astype(F32)[:, 0:1, :]
        st = []
        for d in group:
            q_e, q_l = qd[d, 0, 0:ROWS, :], qd[d, 0, ROWS : 2 * ROWS, :]
            g_e, g_l = qd[d, 1, 0:ROWS, :], qd[d, 1, ROWS : 2 * ROWS, :]
            span_q = meta[d, 2:3, 0:DIM]
            low = jnp.where(span_k < span_q[None], 1.0, 0.0)
            low_rows = jnp.broadcast_to(low, (SIDE, SPAN, DIM)).reshape(KEYS, DIM)
            high_rows = 1.0 - low_rows
            low_wide = jnp.concatenate([low, low], axis=2)
            low_b, high_b = low_rows.astype(BF16), high_rows.astype(BF16)
            k_cat = jnp.concatenate([k_e * low_b, k_l * high_b], axis=1)
            v_cat = jnp.concatenate([v_e * low_b, v_l * high_b], axis=1)
            s1 = dot_nn(k_e, qt[d, 0, 128:256, :])
            p1 = dot_nn(v_e, qt[d, 1, 128:256, :])
            s2 = dot_nn(k_cat, qt[d, 0])
            p2 = dot_nn(v_cat, qt[d, 1])
            st.append((d, low_rows, high_rows, low_wide, k_cat, s1, p1, s2, p2, q_e, q_l, g_e, g_l))
        tot = None
        for (d, low_rows, high_rows, low_wide, k_cat, s1, p1, s2, p2, q_e, q_l, g_e, g_l) in st:
            lse_e, lse_l = meta[d, 0:1, 0:ROWS], meta[d, 0:1, ROWS : 2 * ROWS]
            del_e, del_l = meta[d, 1:2, 0:ROWS], meta[d, 1:2, ROWS : 2 * ROWS]
            probs = probs_of(s1, lse_l)
            grad_scores = (probs * (p1 - del_l)).astype(BF16)
            dv_e = dot_nn(probs.astype(BF16), g_l)
            dk_e = dot_nn(grad_scores, q_l)
            dq_l = dot_tn(k_e, grad_scores)
            q_cat = jnp.concatenate([q_e, q_l], axis=1)
            g_cat = jnp.concatenate([g_e, g_l], axis=1)
            lse = jnp.where(low_wide > 0.5, lse_e[None], lse_l[None])
            delta = jnp.where(low_wide > 0.5, del_e[None], del_l[None])
            scores = s2.reshape(SIDE, SPAN, ROWS) * (SCALE * LOG2E) - lse
            row_k = lax.broadcasted_iota(jnp.int32, (SPAN, ROWS), 0)
            col_r = lax.broadcasted_iota(jnp.int32, (SPAN, ROWS), 1) // GROUP
            seen = row_k <= col_r + jnp.where(own, 0, SPAN)
            first = jnp.where(seen, scores[0], -1e30)
            scores = jnp.concatenate([first[None], scores[1:]], axis=0)
            probs = jnp.exp2(scores)
            grad_probs = p2.reshape(SIDE, SPAN, ROWS)
            grad_scores = (probs * (grad_probs - delta)).astype(BF16).reshape(KEYS, ROWS)
            probs = probs.astype(BF16).reshape(KEYS, ROWS)
            dv = dot_nn(probs, g_cat)
            dk = dot_nn(grad_scores, q_cat)
            dq = dot_tn(k_cat, grad_scores)
            dqt[d, 0:128, :] += dq[0:128]
            dqt[d, 128:256, :] += dq[128:256] + dq_l
            parts = [dk_e + dk[:, 0:128] * low_rows, dk[:, 128:256] * high_rows, dv_e + dv[:, 0:128] * low_rows, dv[:, 128:256] * high_rows]
            tot = parts if tot is None else [x + y for x, y in zip(tot, parts)]
            own = False
        for n in range(4):
            acc[slots, SPAN * n : SPAN * (n + 1), :] += tot[n].reshape(SIDE, SPAN, DIM)

    def send_y(c):
        if c:
            lpart[c - 1] = acc[SIDE * c : SIDE * (c + 1), 192:256].astype(BF16)
            rz_last[c].start()
        for n in (2, 1, 3):
            part[c, n - 1, 0:192] = acc[SIDE * c + n, 0:192].astype(BF16)
            ry_most[c][n - 1].start()

    def sum_y(c):
        arrive(ry_most[c])
        total = acc[SIDE * c, 0:192]
        for n in range(SIDE - 1):
            total = total + ybuf[c, n, 0:192].astype(F32)
        return total

    def send_z(c):
        zpart[c - 1] = sum_y(c).astype(BF16)
        rz_most[c].start()

    def turn_last():
        arrive(rz_last[1:])
        for n in (2, 1, 3, 0):
            total = acc[n, 192:256]
            for s in range(SIDE - 1):
                total = total + lbuf[s, n].astype(F32)
            if n:
                part[0, n - 1, 192:256] = total.astype(BF16)
                ry_last[n - 1].start()
            else:
                acc[0, 192:256] = total

    def send_x(d):
        xpart[d - 1] = dqt[d].astype(BF16)
        rx_go[d].start()

    def pick(i, table):
        value = jnp.int32(table[-1])
        for n, entry in enumerate(table[:-1]):
            value = jnp.where(i == n, entry, value)
        return value

    def finish_x():
        arrive(rx_go[1:])
        total = dqt[0]
        for n in range(SIDE - 1):
            total = total + xbuf[n].astype(F32)
        total = total * SCALE
        out[0:ROWS, :] = total[0:128].T.astype(BF16)
        out[ROWS : 2 * ROWS, :] = total[128:256].T.astype(BF16)

    def finish_kv():
        most_sum = sum_y(0)
        arrive(rz_most[1:])
        for n in range(SIDE - 1):
            most_sum = most_sum + zbuf[n].astype(F32)
        out[512:640, :] = (most_sum[0:128] * SCALE).astype(BF16)
        out[640:704, :] = most_sum[128:192].astype(BF16)
        arrive(ry_last)
        last_sum = acc[0, 192:256]
        for n in range(SIDE - 1):
            last_sum = last_sum + ybuf[0, n, 192:256].astype(F32)
        out[704:768, :] = last_sum.astype(BF16)

    def need_y(c):
        arrive(y_head[c])
        if c:
            arrive([z_tail[n][c - 1] for n in range(SIDE)])

    def need_q(d):
        arrive(q_come[d] + [meta_go[d]])
        turn(d)

    actions = {
        "need_y": need_y,
        "need_q": need_q,
        "send_y": send_y,
        "send_z": send_z,
        "send_x": send_x,
    }

    def act(names):
        for name in names:
            actions[name[:-1]](int(name[-1]))

    def loop_step(i, carry):
        for n in BEFORE:
            pl.when(i == n)(lambda n=n: act(BEFORE[n]))
        c = pick(i, [entry[1] for entry in ORDER])
        for group in GROUPS:
            chosen = pick(i, [int(entry[0] == group) for entry in ORDER])
            pl.when(chosen == 1)(lambda group=group: step(GROUPS[group], c, i == 0))
        for n in AFTER:
            pl.when(i == n)(lambda n=n: act(AFTER[n]))
        return carry

    turn(0)
    need_y(0)
    own_early()
    lax.fori_loop(0, len(ORDER), loop_step, 0)
    act(LAST)
    sent(links.made[:45])
    turn_last()
    sent(ry_most[1] + ry_most[3] + rz_last[1:] + rx_go[1:2] + rx_go[3:4] + [rz_most[1], rz_most[3]])
    send_z(2)
    sent(ry_most[2] + ry_most[0] + [rx_go[2]])
    finish_x()
    sent(ry_last)
    finish_kv()
    sent([rz_most[2]])


COPIES = 3 + 12 + 3 + 12 + 8 + 4 + 3 + 12 + 3 + 3 + 3 + 3
GROUPS = {"t": (0, 1, 3), "s": (2,), "q": (0, 1, 2, 3)}
ORDER = (("t", 0), ("t", 1), ("t", 3), ("s", 1), ("s", 3), ("q", 2), ("s", 0))
BEFORE = {0: ("need_q1", "need_q3"), 1: ("need_y1",), 2: ("need_y3",), 3: ("need_q2",), 5: ("need_y2",)}
AFTER = {3: ("send_y1",), 4: ("send_y3",), 5: ("send_y2", "send_x1", "send_x3", "send_z1")}
LAST = ("send_x2", "send_y0", "send_z3")


def body(queries, keys, values, grad_out, saved_stats, positions):
    hbm_spec = pl.BlockSpec(memory_space=pltpu.HBM)
    vmem_spec = pl.BlockSpec(memory_space=pltpu.VMEM)
    grads = pl.pallas_call(
        kernel,
        out_shape=jax.ShapeDtypeStruct((768, DIM), BF16),
        in_specs=[hbm_spec] * 6,
        out_specs=vmem_spec,
        scratch_shapes=[
            pltpu.VMEM((4, 2, 512, DIM), BF16),
            pltpu.VMEM((16, 272, DIM), BF16),
            pltpu.VMEM((4, 8, 512), F32),
            pltpu.VMEM((8, 128), F32),
            pltpu.VMEM((1, 128), jnp.int32),
            pltpu.VMEM((4, 2, 256, ROWS), BF16),
            pltpu.VMEM((16, 256, DIM), F32),
            pltpu.VMEM((4, 256, ROWS), F32),
            pltpu.VMEM((4, 3, 256, DIM), BF16),
            pltpu.VMEM((4, 3, 256, DIM), BF16),
            pltpu.VMEM((3, 192, DIM), BF16),
            pltpu.VMEM((3, 192, DIM), BF16),
            pltpu.VMEM((3, 4, 64, DIM), BF16),
            pltpu.VMEM((3, 4, 64, DIM), BF16),
            pltpu.VMEM((3, 256, ROWS), BF16),
            pltpu.VMEM((3, 256, ROWS), BF16),
            pltpu.SemaphoreType.DMA((7,)),
            pltpu.SemaphoreType.DMA((COPIES,)),
            pltpu.SemaphoreType.DMA((COPIES,)),
        ],
        compiler_params=pltpu.CompilerParams(
            collective_id=0, has_side_effects=True, vmem_limit_bytes=62 * 1024 * 1024
        ),
    )(
        queries.reshape(512, DIM),
        keys.reshape(128, DIM),
        values.reshape(128, DIM),
        grad_out.reshape(512, DIM),
        saved_stats.reshape(8, 128),
        positions.reshape(1, 128),
    )
    return (
        grads[0:512].reshape(128, GROUP, DIM),
        grads[512:640].reshape(128, 1, DIM),
        grads[640:768].reshape(128, 1, DIM),
    )


def solution(mesh):
    in_specs = (
        P("ctx", "tp", None),
        P("ctx", "tp", None),
        P("ctx", "tp", None),
        P("ctx", "tp", None),
        P(None, "tp", "ctx"),
        P("ctx"),
    )
    out_specs = (P("ctx", "tp", None), P("ctx", "tp", None), P("ctx", "tp", None))
    return jax.shard_map(body, mesh=mesh, in_specs=in_specs, out_specs=out_specs, check_vma=False)
```

```python
import math

import jax
import jax.numpy as jnp
from jax import lax
from jax.experimental import pallas as pl
from jax.experimental.pallas import tpu as pltpu
from jax.sharding import PartitionSpec as P

SIDE = 4
SPAN = 64
DIM = 128
GROUP = 4
ROWS = SPAN * GROUP
KEYS = SPAN * SIDE
LOG2E = 1.4426950408889634
SCALE = 1.0 / math.sqrt(DIM)
F32 = jnp.float32
BF16 = jnp.bfloat16
MESH = pl.DeviceIdType.MESH


def dot_nt(a, b):
    return lax.dot_general(a, b, (((1,), (1,)), ((), ())), preferred_element_type=F32)


def dot_tn(a, b):
    return lax.dot_general(a, b, (((0,), (0,)), ((), ())), preferred_element_type=F32)


def dot_nn(a, b):
    return jnp.dot(a, b, preferred_element_type=F32)


class Links:
    def __init__(self, send_sems, recv_sems):
        self.send_sems = send_sems
        self.recv_sems = recv_sems
        self.count = 0
        self.made = []

    def copy(self, src, dst, device):
        made = pltpu.make_async_remote_copy(
            src_ref=src,
            dst_ref=dst,
            send_sem=self.send_sems.at[self.count],
            recv_sem=self.recv_sems.at[self.count],
            device_id={"ctx": device},
            device_id_type=MESH,
        )
        self.count += 1
        self.made.append(made)
        return made


def kernel(
    q_in, k_in, v_in, g_in, st_in, pos_in,
    out,
    qd, kv, meta, stats, pos, qt, acc, dqt,
    part, ybuf, zpart, zbuf, lpart, lbuf, xpart, xbuf,
    local_sems, send_sems, recv_sems,
):
    me = lax.axis_index("ctx")
    z, x, y = me // (SIDE * SIDE), (me // SIDE) % SIDE, me % SIDE

    def at(dz=0, dx=0, dy=0):
        return (
            ((z + dz) % SIDE) * (SIDE * SIDE) + ((x + dx) % SIDE) * SIDE + (y + dy) % SIDE
        )

    peers = [at(dx=1), at(dx=2), at(dx=3), at(dy=1), at(dy=2), at(dy=3), at(dz=1), at(dz=2), at(dz=3)]

    loads = [
        pltpu.make_async_copy(q_in, qd.at[0, 0], local_sems.at[0]),
        pltpu.make_async_copy(g_in, qd.at[0, 1], local_sems.at[1]),
        pltpu.make_async_copy(k_in, kv.at[0, pl.ds(0, 128)], local_sems.at[2]),
        pltpu.make_async_copy(v_in.at[pl.ds(0, 64)], kv.at[0, pl.ds(128, 64)], local_sems.at[3]),
        pltpu.make_async_copy(v_in.at[pl.ds(64, 64)], kv.at[0, pl.ds(208, 64)], local_sems.at[6]),
        pltpu.make_async_copy(st_in, stats, local_sems.at[4]),
        pltpu.make_async_copy(pos_in, pos, local_sems.at[5]),
    ]
    for load in loads:
        load.start()
    barrier = pltpu.get_barrier_semaphore()
    for peer in peers:
        pl.semaphore_signal(barrier, inc=1, device_id={"ctx": peer}, device_id_type=MESH)

    for load in loads[2:5] + loads[6:]:
        load.wait()
    span = (pos[0:1, 0:1] // SPAN).astype(F32)
    kv[0, 192:208, :] = jnp.broadcast_to(span, (16, DIM)).astype(BF16)

    links = Links(send_sems, recv_sems)
    head, tail = pl.ds(0, 208), pl.ds(208, 64)
    z_head = [None] + [
        links.copy(kv.at[0, head], kv.at[SIDE * s, head], at(dz=SIDE - s)) for s in range(1, SIDE)
    ]
    z_tail = [None] + [
        [
            links.copy(kv.at[n, tail], kv.at[SIDE * s + n, tail], at(dz=SIDE - s))
            for s in range(1, SIDE)
        ]
        for n in range(1, SIDE)
    ]
    z_tail[0] = [
        links.copy(kv.at[0, tail], kv.at[SIDE * s, tail], at(dz=SIDE - s)) for s in range(1, SIDE)
    ]
    y_tail = [None] + [
        links.copy(kv.at[0, tail], kv.at[s, tail], at(dy=SIDE - s)) for s in range(1, SIDE)
    ]
    y_head = [
        [
            links.copy(kv.at[SIDE * c, head], kv.at[SIDE * c + s, head], at(dy=SIDE - s))
            for s in range(1, SIDE)
        ]
        for c in range(SIDE)
    ]
    halves = (pl.ds(0, ROWS), pl.ds(ROWS, ROWS))
    q_right = [
        [links.copy(qd.at[0, n, h], qd.at[3, n, h], at(dx=1)) for h in halves] for n in range(2)
    ]
    q_left = [
        [links.copy(qd.at[0, n, h], qd.at[1, n, h], at(dx=3)) for h in halves] for n in range(2)
    ]
    on_right = [links.copy(qd.at[3, 0, h], qd.at[2, 0, h], at(dx=1)) for h in halves]
    on_left = [links.copy(qd.at[1, 1, h], qd.at[2, 1, h], at(dx=3)) for h in halves]
    meta_go = [None] + [
        links.copy(meta.at[0], meta.at[s], at(dx=SIDE - s)) for s in range(1, SIDE)
    ]
    q_come = [None, q_left[0], on_right + on_left, q_right[1]]
    most, last = pl.ds(0, 192), pl.ds(192, 64)
    ry_most = [
        [
            links.copy(part.at[c, s - 1, most], ybuf.at[c, s - 1, most], at(dy=s))
            for s in range(1, SIDE)
        ]
        for c in range(SIDE)
    ]
    ry_last = [
        links.copy(part.at[0, s - 1, last], ybuf.at[0, s - 1, last], at(dy=s))
        for s in range(1, SIDE)
    ]
    rz_most = [None] + [
        links.copy(zpart.at[s - 1], zbuf.at[s - 1], at(dz=s)) for s in range(1, SIDE)
    ]
    rz_last = [None] + [
        links.copy(lpart.at[s - 1], lbuf.at[s - 1], at(dz=s)) for s in range(1, SIDE)
    ]
    rx_go = [None] + [
        links.copy(xpart.at[s - 1], xbuf.at[s - 1], at(dx=s)) for s in range(1, SIDE)
    ]

    def start(copies):
        for copy in copies:
            copy.start()

    def sent(copies):
        for copy in copies:
            copy.wait_send()

    def arrive(copies):
        for copy in copies:
            copy.wait_recv()

    pl.semaphore_wait(barrier, len(peers))
    start((z_head[1], z_head[3]))
    start(y_tail[1:])
    start(y_head[0])
    for load in loads[0:2]:
        load.wait()
    for h in range(2):
        start((q_right[0][h], q_left[1][h]))
    for h in range(2):
        start((q_right[1][h], q_left[0][h]))

    loads[5].wait()
    spread_t = lax.broadcasted_iota(jnp.int32, (128, 512), 0)
    spread_r = lax.broadcasted_iota(jnp.int32, (128, 512), 1)
    spread = jnp.where(spread_r // GROUP == spread_t, 1.0, 0.0).astype(F32)
    wide = jnp.dot(
        stats[...], spread, preferred_element_type=F32, precision=lax.Precision.HIGHEST
    )
    head_of = lax.broadcasted_iota(jnp.int32, (8, 512), 0) % GROUP
    lane_of = lax.broadcasted_iota(jnp.int32, (8, 512), 1) % GROUP
    wide = jnp.where(head_of == lane_of, wide, 0.0)
    meta[0, 0:1, :] = jnp.sum(wide[0:4], axis=0, keepdims=True) * LOG2E
    meta[0, 1:2, :] = jnp.sum(wide[4:8], axis=0, keepdims=True)
    meta[0, 2:3, :] = jnp.broadcast_to(span, (1, 512))
    meta[0, 3:8, :] = jnp.zeros((5, 512), F32)
    start(meta_go[1:])

    def forward_q(h):
        arrive([q_right[0][h]])
        start([on_right[h]])
        arrive([q_left[1][h]])
        start([on_left[h]])

    def forward_z(c):
        arrive([z_head[c]])
        start(y_head[c])

    def forward_y(n):
        arrive([y_tail[n]])
        start(z_tail[n])

    forward_z(1)
    start([z_head[2]])
    forward_z(3)
    start(z_tail[0])
    forward_y(1)
    forward_y(3)
    forward_y(2)
    forward_z(2)
    forward_q(0)
    forward_q(1)

    acc[...] = jnp.zeros_like(acc)
    dqt[...] = jnp.zeros_like(dqt)

    def probs_of(scores, log_total):
        return jnp.exp2(scores * (SCALE * LOG2E) - log_total)

    def turn(d):
        for n in range(2):
            qt[d, n, 0:128, :] = qd[d, n, 0:ROWS, :].T
            qt[d, n, 128:256, :] = qd[d, n, ROWS : 2 * ROWS, :].T

    def own_early():
        key, value = kv[0, 0:64, :], kv[0, 128:192, :]
        query, grad = qd[0, 0, 0:ROWS, :], qd[0, 1, 0:ROWS, :]
        row_k = lax.broadcasted_iota(jnp.int32, (SPAN, ROWS), 0)
        col_r = lax.broadcasted_iota(jnp.int32, (SPAN, ROWS), 1) // GROUP
        scores = dot_nt(key, query) * (SCALE * LOG2E) - meta[0, 0:1, 0:ROWS]
        probs = jnp.exp2(jnp.where(row_k <= col_r, scores, -1e30))
        grad_probs = dot_nt(value, grad)
        grad_scores = (probs * (grad_probs - meta[0, 1:2, 0:ROWS])).astype(BF16)
        acc[0, 128:192, :] += dot_nn(probs.astype(BF16), grad)
        acc[0, 0:64, :] += dot_nn(grad_scores, query)
        dqt[0, 0:128, :] += dot_tn(key, grad_scores)

    def step(group, c, own):
        base = SIDE * c
        slots = pl.ds(base, SIDE)

        def rows(start):
            return kv[slots, start : start + SPAN, :].reshape(KEYS, DIM)

        k_e, k_l, v_e, v_l = rows(0), rows(64), rows(128), rows(208)
        span_k = kv[slots, 192:208, :].astype(F32)[:, 0:1, :]
        st = []
        for d in group:
            q_e, q_l = qd[d, 0, 0:ROWS, :], qd[d, 0, ROWS : 2 * ROWS, :]
            g_e, g_l = qd[d, 1, 0:ROWS, :], qd[d, 1, ROWS : 2 * ROWS, :]
            span_q = meta[d, 2:3, 0:DIM]
            low = jnp.where(span_k < span_q[None], 1.0, 0.0)
            low_rows = jnp.broadcast_to(low, (SIDE, SPAN, DIM)).reshape(KEYS, DIM)
            high_rows = 1.0 - low_rows
            low_wide = jnp.concatenate([low, low], axis=2)
            low_b, high_b = low_rows.astype(BF16), high_rows.astype(BF16)
            k_cat = jnp.concatenate([k_e * low_b, k_l * high_b], axis=1)
            v_cat = jnp.concatenate([v_e * low_b, v_l * high_b], axis=1)
            s1 = dot_nn(k_e, qt[d, 0, 128:256, :])
            p1 = dot_nn(v_e, qt[d, 1, 128:256, :])
            s2 = dot_nn(k_cat, qt[d, 0])
            p2 = dot_nn(v_cat, qt[d, 1])
            st.append((d, low_rows, high_rows, low_wide, k_cat, s1, p1, s2, p2, q_e, q_l, g_e, g_l))
        tot = None
        for (d, low_rows, high_rows, low_wide, k_cat, s1, p1, s2, p2, q_e, q_l, g_e, g_l) in st:
            lse_e, lse_l = meta[d, 0:1, 0:ROWS], meta[d, 0:1, ROWS : 2 * ROWS]
            del_e, del_l = meta[d, 1:2, 0:ROWS], meta[d, 1:2, ROWS : 2 * ROWS]
            probs = probs_of(s1, lse_l)
            grad_scores = (probs * (p1 - del_l)).astype(BF16)
            dv_e = dot_nn(probs.astype(BF16), g_l)
            dk_e = dot_nn(grad_scores, q_l)
            dq_l = dot_tn(k_e, grad_scores)
            q_cat = jnp.concatenate([q_e, q_l], axis=1)
            g_cat = jnp.concatenate([g_e, g_l], axis=1)
            lse = jnp.where(low_wide > 0.5, lse_e[None], lse_l[None])
            delta = jnp.where(low_wide > 0.5, del_e[None], del_l[None])
            scores = s2.reshape(SIDE, SPAN, ROWS) * (SCALE * LOG2E) - lse
            row_k = lax.broadcasted_iota(jnp.int32, (SPAN, ROWS), 0)
            col_r = lax.broadcasted_iota(jnp.int32, (SPAN, ROWS), 1) // GROUP
            seen = row_k <= col_r + jnp.where(own, 0, SPAN)
            first = jnp.where(seen, scores[0], -1e30)
            scores = jnp.concatenate([first[None], scores[1:]], axis=0)
            probs = jnp.exp2(scores)
            grad_probs = p2.reshape(SIDE, SPAN, ROWS)
            grad_scores = (probs * (grad_probs - delta)).astype(BF16).reshape(KEYS, ROWS)
            probs = probs.astype(BF16).reshape(KEYS, ROWS)
            dv = dot_nn(probs, g_cat)
            dk = dot_nn(grad_scores, q_cat)
            dq = dot_tn(k_cat, grad_scores)
            dqt[d, 0:128, :] += dq[0:128]
            dqt[d, 128:256, :] += dq[128:256] + dq_l
            parts = [dk_e + dk[:, 0:128] * low_rows, dk[:, 128:256] * high_rows, dv_e + dv[:, 0:128] * low_rows, dv[:, 128:256] * high_rows]
            tot = parts if tot is None else [x + y for x, y in zip(tot, parts)]
            own = False
        for n in range(4):
            acc[slots, SPAN * n : SPAN * (n + 1), :] += tot[n].reshape(SIDE, SPAN, DIM)

    def send_y(c):
        if c:
            lpart[c - 1] = acc[SIDE * c : SIDE * (c + 1), 192:256].astype(BF16)
            rz_last[c].start()
        for n in (2, 1, 3):
            part[c, n - 1, 0:192] = acc[SIDE * c + n, 0:192].astype(BF16)
            ry_most[c][n - 1].start()

    def sum_y(c):
        arrive(ry_most[c])
        total = acc[SIDE * c, 0:192]
        for n in range(SIDE - 1):
            total = total + ybuf[c, n, 0:192].astype(F32)
        return total

    def send_z(c):
        zpart[c - 1] = sum_y(c).astype(BF16)
        rz_most[c].start()

    def turn_last():
        arrive(rz_last[1:])
        for n in (2, 1, 3, 0):
            total = acc[n, 192:256]
            for s in range(SIDE - 1):
                total = total + lbuf[s, n].astype(F32)
            if n:
                part[0, n - 1, 192:256] = total.astype(BF16)
                ry_last[n - 1].start()
            else:
                acc[0, 192:256] = total

    def send_x(d):
        xpart[d - 1] = dqt[d].astype(BF16)
        rx_go[d].start()

    def pick(i, table):
        value = jnp.int32(table[-1])
        for n, entry in enumerate(table[:-1]):
            value = jnp.where(i == n, entry, value)
        return value

    def finish_x():
        arrive(rx_go[1:])
        total = dqt[0]
        for n in range(SIDE - 1):
            total = total + xbuf[n].astype(F32)
        total = total * SCALE
        out[0:ROWS, :] = total[0:128].T.astype(BF16)
        out[ROWS : 2 * ROWS, :] = total[128:256].T.astype(BF16)

    def finish_kv():
        most_sum = sum_y(0)
        arrive(rz_most[1:])
        for n in range(SIDE - 1):
            most_sum = most_sum + zbuf[n].astype(F32)
        out[512:640, :] = (most_sum[0:128] * SCALE).astype(BF16)
        out[640:704, :] = most_sum[128:192].astype(BF16)
        arrive(ry_last)
        last_sum = acc[0, 192:256]
        for n in range(SIDE - 1):
            last_sum = last_sum + ybuf[0, n, 192:256].astype(F32)
        out[704:768, :] = last_sum.astype(BF16)

    def need_y(c):
        arrive(y_head[c])
        if c:
            arrive([z_tail[n][c - 1] for n in range(SIDE)])

    def need_q(d):
        arrive(q_come[d] + [meta_go[d]])
        turn(d)

    actions = {
        "need_y": need_y,
        "need_q": need_q,
        "send_y": send_y,
        "send_z": send_z,
        "send_x": send_x,
    }

    def act(names):
        for name in names:
            actions[name[:-1]](int(name[-1]))

    def loop_step(i, carry):
        for n in BEFORE:
            pl.when(i == n)(lambda n=n: act(BEFORE[n]))
        c = pick(i, [entry[1] for entry in ORDER])
        for group in GROUPS:
            chosen = pick(i, [int(entry[0] == group) for entry in ORDER])
            pl.when(chosen == 1)(lambda group=group: step(GROUPS[group], c, i == 0))
        for n in AFTER:
            pl.when(i == n)(lambda n=n: act(AFTER[n]))
        return carry

    turn(0)
    need_y(0)
    own_early()
    lax.fori_loop(0, len(ORDER), loop_step, 0)
    act(LAST)
    sent(links.made[:45])
    turn_last()
    sent(ry_most[1] + ry_most[3] + rz_last[1:] + rx_go[1:2] + rx_go[3:4] + [rz_most[1], rz_most[3]])
    send_z(2)
    sent(ry_most[2] + ry_most[0] + [rx_go[2]])
    finish_x()
    sent(ry_last)
    finish_kv()
    sent([rz_most[2]])


COPIES = 3 + 12 + 3 + 12 + 8 + 4 + 3 + 12 + 3 + 3 + 3 + 3
GROUPS = {"t": (0, 1, 3), "s": (2,), "q": (0, 1, 2, 3)}
ORDER = (("t", 0), ("t", 1), ("t", 3), ("s", 1), ("s", 3), ("q", 2), ("s", 0))
BEFORE = {0: ("need_q1", "need_q3"), 1: ("need_y1",), 2: ("need_y3",), 3: ("need_q2",), 5: ("need_y2",)}
AFTER = {3: ("send_y1",), 4: ("send_y3",), 5: ("send_y2", "send_x1", "send_x3")}
LAST = ("send_y0", "send_x2", "send_z1", "send_z3")


def body(queries, keys, values, grad_out, saved_stats, positions):
    hbm_spec = pl.BlockSpec(memory_space=pltpu.HBM)
    vmem_spec = pl.BlockSpec(memory_space=pltpu.VMEM)
    grads = pl.pallas_call(
        kernel,
        out_shape=jax.ShapeDtypeStruct((768, DIM), BF16),
        in_specs=[hbm_spec] * 6,
        out_specs=vmem_spec,
        scratch_shapes=[
            pltpu.VMEM((4, 2, 512, DIM), BF16),
            pltpu.VMEM((16, 272, DIM), BF16),
            pltpu.VMEM((4, 8, 512), F32),
            pltpu.VMEM((8, 128), F32),
            pltpu.VMEM((1, 128), jnp.int32),
            pltpu.VMEM((4, 2, 256, ROWS), BF16),
            pltpu.VMEM((16, 256, DIM), F32),
            pltpu.VMEM((4, 256, ROWS), F32),
            pltpu.VMEM((4, 3, 256, DIM), BF16),
            pltpu.VMEM((4, 3, 256, DIM), BF16),
            pltpu.VMEM((3, 192, DIM), BF16),
            pltpu.VMEM((3, 192, DIM), BF16),
            pltpu.VMEM((3, 4, 64, DIM), BF16),
            pltpu.VMEM((3, 4, 64, DIM), BF16),
            pltpu.VMEM((3, 256, ROWS), BF16),
            pltpu.VMEM((3, 256, ROWS), BF16),
            pltpu.SemaphoreType.DMA((7,)),
            pltpu.SemaphoreType.DMA((COPIES,)),
            pltpu.SemaphoreType.DMA((COPIES,)),
        ],
        compiler_params=pltpu.CompilerParams(
            collective_id=0, has_side_effects=True, vmem_limit_bytes=62 * 1024 * 1024
        ),
    )(
        queries.reshape(512, DIM),
        keys.reshape(128, DIM),
        values.reshape(128, DIM),
        grad_out.reshape(512, DIM),
        saved_stats.reshape(8, 128),
        positions.reshape(1, 128),
    )
    return (
        grads[0:512].reshape(128, GROUP, DIM),
        grads[512:640].reshape(128, 1, DIM),
        grads[640:768].reshape(128, 1, DIM),
    )


def solution(mesh):
    in_specs = (
        P("ctx", "tp", None),
        P("ctx", "tp", None),
        P("ctx", "tp", None),
        P("ctx", "tp", None),
        P(None, "tp", "ctx"),
        P("ctx"),
    )
    out_specs = (P("ctx", "tp", None), P("ctx", "tp", None), P("ctx", "tp", None))
    return jax.shard_map(body, mesh=mesh, in_specs=in_specs, out_specs=out_specs, check_vma=False)
```

```python
import math

import jax
import jax.numpy as jnp
from jax import lax
from jax.experimental import pallas as pl
from jax.experimental.pallas import tpu as pltpu
from jax.sharding import PartitionSpec as P

SIDE = 4
SPAN = 64
DIM = 128
GROUP = 4
ROWS = SPAN * GROUP
KEYS = SPAN * SIDE
LOG2E = 1.4426950408889634
SCALE = 1.0 / math.sqrt(DIM)
F32 = jnp.float32
BF16 = jnp.bfloat16
MESH = pl.DeviceIdType.MESH


def dot_nt(a, b):
    return lax.dot_general(a, b, (((1,), (1,)), ((), ())), preferred_element_type=F32)


def dot_tn(a, b):
    return lax.dot_general(a, b, (((0,), (0,)), ((), ())), preferred_element_type=F32)


def dot_nn(a, b):
    return jnp.dot(a, b, preferred_element_type=F32)


class Links:
    def __init__(self, send_sems, recv_sems):
        self.send_sems = send_sems
        self.recv_sems = recv_sems
        self.count = 0
        self.made = []

    def copy(self, src, dst, device):
        made = pltpu.make_async_remote_copy(
            src_ref=src,
            dst_ref=dst,
            send_sem=self.send_sems.at[self.count],
            recv_sem=self.recv_sems.at[self.count],
            device_id={"ctx": device},
            device_id_type=MESH,
        )
        self.count += 1
        self.made.append(made)
        return made


def kernel(
    q_in, k_in, v_in, g_in, st_in, pos_in,
    out,
    qd, kv, meta, stats, pos, qt, acc, dqt,
    part, ybuf, zpart, zbuf, lpart, lbuf, xpart, xbuf,
    local_sems, send_sems, recv_sems,
):
    me = lax.axis_index("ctx")
    z, x, y = me // (SIDE * SIDE), (me // SIDE) % SIDE, me % SIDE

    def at(dz=0, dx=0, dy=0):
        return (
            ((z + dz) % SIDE) * (SIDE * SIDE) + ((x + dx) % SIDE) * SIDE + (y + dy) % SIDE
        )

    peers = [at(dx=1), at(dx=2), at(dx=3), at(dy=1), at(dy=2), at(dy=3), at(dz=1), at(dz=2), at(dz=3)]

    loads = [
        pltpu.make_async_copy(q_in, qd.at[0, 0], local_sems.at[0]),
        pltpu.make_async_copy(g_in, qd.at[0, 1], local_sems.at[1]),
        pltpu.make_async_copy(k_in, kv.at[0, pl.ds(0, 128)], local_sems.at[2]),
        pltpu.make_async_copy(v_in.at[pl.ds(0, 64)], kv.at[0, pl.ds(128, 64)], local_sems.at[3]),
        pltpu.make_async_copy(v_in.at[pl.ds(64, 64)], kv.at[0, pl.ds(208, 64)], local_sems.at[6]),
        pltpu.make_async_copy(st_in, stats, local_sems.at[4]),
        pltpu.make_async_copy(pos_in, pos, local_sems.at[5]),
    ]
    for load in loads:
        load.start()
    barrier = pltpu.get_barrier_semaphore()
    for peer in peers:
        pl.semaphore_signal(barrier, inc=1, device_id={"ctx": peer}, device_id_type=MESH)

    for load in loads[2:5] + loads[6:]:
        load.wait()
    span = (pos[0:1, 0:1] // SPAN).astype(F32)
    kv[0, 192:208, :] = jnp.broadcast_to(span, (16, DIM)).astype(BF16)

    links = Links(send_sems, recv_sems)
    head, tail = pl.ds(0, 208), pl.ds(208, 64)
    z_head = [None] + [
        links.copy(kv.at[0, head], kv.at[SIDE * s, head], at(dz=SIDE - s)) for s in range(1, SIDE)
    ]
    z_tail = [None] + [
        [
            links.copy(kv.at[n, tail], kv.at[SIDE * s + n, tail], at(dz=SIDE - s))
            for s in range(1, SIDE)
        ]
        for n in range(1, SIDE)
    ]
    z_tail[0] = [
        links.copy(kv.at[0, tail], kv.at[SIDE * s, tail], at(dz=SIDE - s)) for s in range(1, SIDE)
    ]
    y_tail = [None] + [
        links.copy(kv.at[0, tail], kv.at[s, tail], at(dy=SIDE - s)) for s in range(1, SIDE)
    ]
    y_head = [
        [
            links.copy(kv.at[SIDE * c, head], kv.at[SIDE * c + s, head], at(dy=SIDE - s))
            for s in range(1, SIDE)
        ]
        for c in range(SIDE)
    ]
    halves = (pl.ds(0, ROWS), pl.ds(ROWS, ROWS))
    q_right = [
        [links.copy(qd.at[0, n, h], qd.at[3, n, h], at(dx=1)) for h in halves] for n in range(2)
    ]
    q_left = [
        [links.copy(qd.at[0, n, h], qd.at[1, n, h], at(dx=3)) for h in halves] for n in range(2)
    ]
    on_right = [links.copy(qd.at[3, 0, h], qd.at[2, 0, h], at(dx=1)) for h in halves]
    on_left = [links.copy(qd.at[1, 1, h], qd.at[2, 1, h], at(dx=3)) for h in halves]
    meta_go = [None] + [
        links.copy(meta.at[0], meta.at[s], at(dx=SIDE - s)) for s in range(1, SIDE)
    ]
    q_come = [None, q_left[0], on_right + on_left, q_right[1]]
    most, last = pl.ds(0, 192), pl.ds(192, 64)
    ry_most = [
        [
            links.copy(part.at[c, s - 1, most], ybuf.at[c, s - 1, most], at(dy=s))
            for s in range(1, SIDE)
        ]
        for c in range(SIDE)
    ]
    ry_last = [
        links.copy(part.at[0, s - 1, last], ybuf.at[0, s - 1, last], at(dy=s))
        for s in range(1, SIDE)
    ]
    rz_most = [None] + [
        links.copy(zpart.at[s - 1], zbuf.at[s - 1], at(dz=s)) for s in range(1, SIDE)
    ]
    rz_last = [None] + [
        links.copy(lpart.at[s - 1], lbuf.at[s - 1], at(dz=s)) for s in range(1, SIDE)
    ]
    rx_go = [None] + [
        links.copy(xpart.at[s - 1], xbuf.at[s - 1], at(dx=s)) for s in range(1, SIDE)
    ]

    def start(copies):
        for copy in copies:
            copy.start()

    def sent(copies):
        for copy in copies:
            copy.wait_send()

    def arrive(copies):
        for copy in copies:
            copy.wait_recv()

    pl.semaphore_wait(barrier, len(peers))
    start((z_head[1], z_head[3]))
    start(y_tail[1:])
    start(y_head[0])
    for load in loads[0:2]:
        load.wait()
    for h in range(2):
        start((q_right[0][h], q_left[1][h]))
    for h in range(2):
        start((q_right[1][h], q_left[0][h]))

    loads[5].wait()
    spread_t = lax.broadcasted_iota(jnp.int32, (128, 512), 0)
    spread_r = lax.broadcasted_iota(jnp.int32, (128, 512), 1)
    spread = jnp.where(spread_r // GROUP == spread_t, 1.0, 0.0).astype(F32)
    wide = jnp.dot(
        stats[...], spread, preferred_element_type=F32, precision=lax.Precision.HIGHEST
    )
    head_of = lax.broadcasted_iota(jnp.int32, (8, 512), 0) % GROUP
    lane_of = lax.broadcasted_iota(jnp.int32, (8, 512), 1) % GROUP
    wide = jnp.where(head_of == lane_of, wide, 0.0)
    meta[0, 0:1, :] = jnp.sum(wide[0:4], axis=0, keepdims=True) * LOG2E
    meta[0, 1:2, :] = jnp.sum(wide[4:8], axis=0, keepdims=True)
    meta[0, 2:3, :] = jnp.broadcast_to(span, (1, 512))
    meta[0, 3:8, :] = jnp.zeros((5, 512), F32)
    start(meta_go[1:])

    def forward_q(h):
        arrive([q_right[0][h]])
        start([on_right[h]])
        arrive([q_left[1][h]])
        start([on_left[h]])

    def forward_z(c):
        arrive([z_head[c]])
        start(y_head[c])

    def forward_y(n):
        arrive([y_tail[n]])
        start(z_tail[n])

    forward_z(1)
    start([z_head[2]])
    forward_z(3)
    start(z_tail[0])
    forward_y(1)
    forward_y(3)
    forward_y(2)
    forward_z(2)
    forward_q(0)
    forward_q(1)

    acc[...] = jnp.zeros_like(acc)
    dqt[...] = jnp.zeros_like(dqt)

    def probs_of(scores, log_total):
        return jnp.exp2(scores * (SCALE * LOG2E) - log_total)

    def turn(d):
        for n in range(2):
            qt[d, n, 0:128, :] = qd[d, n, 0:ROWS, :].T
            qt[d, n, 128:256, :] = qd[d, n, ROWS : 2 * ROWS, :].T

    def own_early():
        key, value = kv[0, 0:64, :], kv[0, 128:192, :]
        query, grad = qd[0, 0, 0:ROWS, :], qd[0, 1, 0:ROWS, :]
        row_k = lax.broadcasted_iota(jnp.int32, (SPAN, ROWS), 0)
        col_r = lax.broadcasted_iota(jnp.int32, (SPAN, ROWS), 1) // GROUP
        scores = dot_nt(key, query) * (SCALE * LOG2E) - meta[0, 0:1, 0:ROWS]
        probs = jnp.exp2(jnp.where(row_k <= col_r, scores, -1e30))
        grad_probs = dot_nt(value, grad)
        grad_scores = (probs * (grad_probs - meta[0, 1:2, 0:ROWS])).astype(BF16)
        acc[0, 128:192, :] += dot_nn(probs.astype(BF16), grad)
        acc[0, 0:64, :] += dot_nn(grad_scores, query)
        dqt[0, 0:128, :] += dot_tn(key, grad_scores)

    def step(group, c, own):
        base = SIDE * c
        slots = pl.ds(base, SIDE)

        def rows(start):
            return kv[slots, start : start + SPAN, :].reshape(KEYS, DIM)

        k_e, k_l, v_e, v_l = rows(0), rows(64), rows(128), rows(208)
        span_k = kv[slots, 192:208, :].astype(F32)[:, 0:1, :]
        st = []
        for d in group:
            q_e, q_l = qd[d, 0, 0:ROWS, :], qd[d, 0, ROWS : 2 * ROWS, :]
            g_e, g_l = qd[d, 1, 0:ROWS, :], qd[d, 1, ROWS : 2 * ROWS, :]
            span_q = meta[d, 2:3, 0:DIM]
            low = jnp.where(span_k < span_q[None], 1.0, 0.0)
            low_rows = jnp.broadcast_to(low, (SIDE, SPAN, DIM)).reshape(KEYS, DIM)
            high_rows = 1.0 - low_rows
            low_wide = jnp.concatenate([low, low], axis=2)
            low_b, high_b = low_rows.astype(BF16), high_rows.astype(BF16)
            k_cat = jnp.concatenate([k_e * low_b, k_l * high_b], axis=1)
            v_cat = jnp.concatenate([v_e * low_b, v_l * high_b], axis=1)
            s1 = dot_nn(k_e, qt[d, 0, 128:256, :])
            p1 = dot_nn(v_e, qt[d, 1, 128:256, :])
            s2 = dot_nn(k_cat, qt[d, 0])
            p2 = dot_nn(v_cat, qt[d, 1])
            st.append((d, low_rows, high_rows, low_wide, k_cat, s1, p1, s2, p2, q_e, q_l, g_e, g_l))
        tot = None
        for (d, low_rows, high_rows, low_wide, k_cat, s1, p1, s2, p2, q_e, q_l, g_e, g_l) in st:
            lse_e, lse_l = meta[d, 0:1, 0:ROWS], meta[d, 0:1, ROWS : 2 * ROWS]
            del_e, del_l = meta[d, 1:2, 0:ROWS], meta[d, 1:2, ROWS : 2 * ROWS]
            probs = probs_of(s1, lse_l)
            grad_scores = (probs * (p1 - del_l)).astype(BF16)
            dv_e = dot_nn(probs.astype(BF16), g_l)
            dk_e = dot_nn(grad_scores, q_l)
            dq_l = dot_tn(k_e, grad_scores)
            q_cat = jnp.concatenate([q_e, q_l], axis=1)
            g_cat = jnp.concatenate([g_e, g_l], axis=1)
            lse = jnp.where(low_wide > 0.5, lse_e[None], lse_l[None])
            delta = jnp.where(low_wide > 0.5, del_e[None], del_l[None])
            scores = s2.reshape(SIDE, SPAN, ROWS) * (SCALE * LOG2E) - lse
            row_k = lax.broadcasted_iota(jnp.int32, (SPAN, ROWS), 0)
            col_r = lax.broadcasted_iota(jnp.int32, (SPAN, ROWS), 1) // GROUP
            seen = row_k <= col_r + jnp.where(own, 0, SPAN)
            first = jnp.where(seen, scores[0], -1e30)
            scores = jnp.concatenate([first[None], scores[1:]], axis=0)
            probs = jnp.exp2(scores)
            grad_probs = p2.reshape(SIDE, SPAN, ROWS)
            grad_scores = (probs * (grad_probs - delta)).astype(BF16).reshape(KEYS, ROWS)
            probs = probs.astype(BF16).reshape(KEYS, ROWS)
            dv = dot_nn(probs, g_cat)
            dk = dot_nn(grad_scores, q_cat)
            dq = dot_tn(k_cat, grad_scores)
            dqt[d, 0:128, :] += dq[0:128]
            dqt[d, 128:256, :] += dq[128:256] + dq_l
            parts = [dk_e + dk[:, 0:128] * low_rows, dk[:, 128:256] * high_rows, dv_e + dv[:, 0:128] * low_rows, dv[:, 128:256] * high_rows]
            tot = parts if tot is None else [x + y for x, y in zip(tot, parts)]
            own = False
        for n in range(4):
            acc[slots, SPAN * n : SPAN * (n + 1), :] += tot[n].reshape(SIDE, SPAN, DIM)

    def send_y(c):
        if c:
            lpart[c - 1] = acc[SIDE * c : SIDE * (c + 1), 192:256].astype(BF16)
            rz_last[c].start()
        for n in (2, 1, 3):
            part[c, n - 1, 0:192] = acc[SIDE * c + n, 0:192].astype(BF16)
            ry_most[c][n - 1].start()

    def sum_y(c):
        arrive(ry_most[c])
        total = acc[SIDE * c, 0:192]
        for n in range(SIDE - 1):
            total = total + ybuf[c, n, 0:192].astype(F32)
        return total

    def send_z(c):
        zpart[c - 1] = sum_y(c).astype(BF16)
        rz_most[c].start()

    def turn_last():
        arrive(rz_last[1:])
        for n in (2, 1, 3, 0):
            total = acc[n, 192:256]
            for s in range(SIDE - 1):
                total = total + lbuf[s, n].astype(F32)
            if n:
                part[0, n - 1, 192:256] = total.astype(BF16)
                ry_last[n - 1].start()
            else:
                acc[0, 192:256] = total

    def send_x(d):
        xpart[d - 1] = dqt[d].astype(BF16)
        rx_go[d].start()

    def pick(i, table):
        value = jnp.int32(table[-1])
        for n, entry in enumerate(table[:-1]):
            value = jnp.where(i == n, entry, value)
        return value

    def finish_x():
        arrive(rx_go[1:])
        total = dqt[0]
        for n in range(SIDE - 1):
            total = total + xbuf[n].astype(F32)
        total = total * SCALE
        out[0:ROWS, :] = total[0:128].T.astype(BF16)
        out[ROWS : 2 * ROWS, :] = total[128:256].T.astype(BF16)

    def finish_kv():
        most_sum = sum_y(0)
        arrive(rz_most[1:])
        for n in range(SIDE - 1):
            most_sum = most_sum + zbuf[n].astype(F32)
        out[512:640, :] = (most_sum[0:128] * SCALE).astype(BF16)
        out[640:704, :] = most_sum[128:192].astype(BF16)
        arrive(ry_last)
        last_sum = acc[0, 192:256]
        for n in range(SIDE - 1):
            last_sum = last_sum + ybuf[0, n, 192:256].astype(F32)
        out[704:768, :] = last_sum.astype(BF16)

    def need_y(c):
        arrive(y_head[c])
        if c:
            arrive([z_tail[n][c - 1] for n in range(SIDE)])

    def need_q(d):
        arrive(q_come[d] + [meta_go[d]])
        turn(d)

    actions = {
        "need_y": need_y,
        "need_q": need_q,
        "send_y": send_y,
        "send_z": send_z,
        "send_x": send_x,
    }

    def act(names):
        for name in names:
            actions[name[:-1]](int(name[-1]))

    def loop_step(i, carry):
        for n in BEFORE:
            pl.when(i == n)(lambda n=n: act(BEFORE[n]))
        c = pick(i, [entry[1] for entry in ORDER])
        for group in GROUPS:
            chosen = pick(i, [int(entry[0] == group) for entry in ORDER])
            pl.when(chosen == 1)(lambda group=group: step(GROUPS[group], c, i == 0))
        for n in AFTER:
            pl.when(i == n)(lambda n=n: act(AFTER[n]))
        return carry

    turn(0)
    need_y(0)
    own_early()
    lax.fori_loop(0, len(ORDER), loop_step, 0)
    act(LAST)
    sent(links.made[:45])
    turn_last()
    sent(ry_most[1] + ry_most[3] + rz_last[1:] + rx_go[1:2] + rx_go[3:4] + [rz_most[1], rz_most[3]])
    send_z(2)
    sent(ry_most[2] + ry_most[0] + [rx_go[2]])
    finish_x()
    sent(ry_last)
    finish_kv()
    sent([rz_most[2]])


COPIES = 3 + 12 + 3 + 12 + 8 + 4 + 3 + 12 + 3 + 3 + 3 + 3
GROUPS = {"t": (0, 1, 3), "s": (2,), "q": (0, 1, 2, 3)}
ORDER = (("t", 0), ("t", 1), ("s", 1), ("t", 3), ("s", 3), ("q", 2), ("s", 0))
BEFORE = {0: ("need_q1", "need_q3"), 1: ("need_y1",), 2: ("need_q2",), 3: ("need_y3",), 5: ("need_y2",)}
AFTER = {2: ("send_y1",), 4: ("send_y3",), 5: ("send_y2", "send_x1", "send_x3", "send_z1")}
LAST = ("send_x2", "send_y0", "send_z3")


def body(queries, keys, values, grad_out, saved_stats, positions):
    hbm_spec = pl.BlockSpec(memory_space=pltpu.HBM)
    vmem_spec = pl.BlockSpec(memory_space=pltpu.VMEM)
    grads = pl.pallas_call(
        kernel,
        out_shape=jax.ShapeDtypeStruct((768, DIM), BF16),
        in_specs=[hbm_spec] * 6,
        out_specs=vmem_spec,
        scratch_shapes=[
            pltpu.VMEM((4, 2, 512, DIM), BF16),
            pltpu.VMEM((16, 272, DIM), BF16),
            pltpu.VMEM((4, 8, 512), F32),
            pltpu.VMEM((8, 128), F32),
            pltpu.VMEM((1, 128), jnp.int32),
            pltpu.VMEM((4, 2, 256, ROWS), BF16),
            pltpu.VMEM((16, 256, DIM), F32),
            pltpu.VMEM((4, 256, ROWS), F32),
            pltpu.VMEM((4, 3, 256, DIM), BF16),
            pltpu.VMEM((4, 3, 256, DIM), BF16),
            pltpu.VMEM((3, 192, DIM), BF16),
            pltpu.VMEM((3, 192, DIM), BF16),
            pltpu.VMEM((3, 4, 64, DIM), BF16),
            pltpu.VMEM((3, 4, 64, DIM), BF16),
            pltpu.VMEM((3, 256, ROWS), BF16),
            pltpu.VMEM((3, 256, ROWS), BF16),
            pltpu.SemaphoreType.DMA((7,)),
            pltpu.SemaphoreType.DMA((COPIES,)),
            pltpu.SemaphoreType.DMA((COPIES,)),
        ],
        compiler_params=pltpu.CompilerParams(
            collective_id=0, has_side_effects=True, vmem_limit_bytes=62 * 1024 * 1024
        ),
    )(
        queries.reshape(512, DIM),
        keys.reshape(128, DIM),
        values.reshape(128, DIM),
        grad_out.reshape(512, DIM),
        saved_stats.reshape(8, 128),
        positions.reshape(1, 128),
    )
    return (
        grads[0:512].reshape(128, GROUP, DIM),
        grads[512:640].reshape(128, 1, DIM),
        grads[640:768].reshape(128, 1, DIM),
    )


def solution(mesh):
    in_specs = (
        P("ctx", "tp", None),
        P("ctx", "tp", None),
        P("ctx", "tp", None),
        P("ctx", "tp", None),
        P(None, "tp", "ctx"),
        P("ctx"),
    )
    out_specs = (P("ctx", "tp", None), P("ctx", "tp", None), P("ctx", "tp", None))
    return jax.shard_map(body, mesh=mesh, in_specs=in_specs, out_specs=out_specs, check_vma=False)
```
